512 devices in a mesh: dp: 16 (over x, y), tensor: 32 (over z, core).
Axes of the slice: x: 4, y: 4, z: 16, core: 2. Of those that a mesh axis runs over, the one named last changes fastest.
Arguments:
- mantissa: bfloat16 [1024, 4096], P('tensor', 'dp'), may hold values from -6 to 6
- block_exponents: int32 [1024, 256], P('tensor'), may hold values from -2 to 3
- norm_gain: bfloat16 [4096], P('dp'), may hold values from 0.099609375 to 1.8984375
- gate_weight: bfloat16 [4096, 14336], P('dp', 'tensor'), may hold values from -0.09375 to 0.09375
- up_weight: bfloat16 [4096, 14336], P('dp', 'tensor'), may hold values from -0.09375 to 0.09375
- down_weight: bfloat16 [14336, 4096], P('tensor', 'dp'), may hold values from -0.046875 to 0.046875
- cotangent: bfloat16 [1024, 4096], P('tensor', 'dp'), may hold values from -6 to 6
Outputs:
- mlp_output: bfloat16 [1024, 4096], P('tensor', 'dp')
- input_grad: bfloat16 [1024, 4096], P('tensor', 'dp')
- grad_gate: float32 [4096, 14336], P('dp', 'tensor')
- grad_up: float32 [4096, 14336], P('dp', 'tensor')
- grad_down: float32 [14336, 4096], P('tensor', 'dp')
The draws below stay inside these ranges and needn't reach their ends.
All inputs are finite; a program needn't handle non-finite values.
Results may differ from the reference program's by a relative error of at most 0.04.
Values may be sent and summed in bfloat16 or wider, within the bound.
A program may use at most 64 MiB of HBM per device.

```python
import jax
import jax.numpy as jnp
from jax import lax

D = 4096
FF = 14336
BLOCK = 16
TOKENS = 1024
N_DP = 16
N_TENSOR = 32


def draw_block_exponents(key, part):
    key = jax.random.fold_in(key, 11)
    blocks = D // BLOCK
    base_draw = jax.random.randint(key, (TOKENS, blocks), -2, 2)
    offset = jnp.arange(blocks, dtype=jnp.int32) * 3 // blocks
    exponents = (base_draw + offset[None, :]).astype(jnp.int32)
    exponents = exponents.at[0, 0].set(-2)
    return exponents.at[0, blocks - 1].set(3)


def block_scale(rng, shape, shards, least, high):
    factor_of, own = 1.0, jax.random.fold_in(rng, 6)
    for dim, blocks in shards:
        steps = jnp.exp(jax.random.uniform(jax.random.fold_in(own, dim), (blocks,), jnp.float32, least / len(shards), high / len(shards)))
        factor_of = factor_of * jnp.repeat(steps, shape[dim] // blocks).reshape([-1 if axis == dim else 1 for axis in range(len(shape))])
    return factor_of


def centred(stream_key, extent, deviation, limit, shards=(), kind=jnp.bfloat16):
    gain = block_scale(stream_key, extent, shards, -0.22, 0.18) if shards else 1.0
    drawn = jax.random.normal(stream_key, extent, jnp.float32) * deviation * gain
    return jnp.minimum(jnp.maximum(drawn, -limit), limit).astype(kind)


def setup_inputs(seed: int = 0) -> dict:
    arg_keys = jax.random.split(jax.random.key(seed), 8)
    return {
        "mantissa": centred(arg_keys[0], (TOKENS, D), 1.0, 6.0, ((0, 32), (1, 16))),
        "block_exponents": draw_block_exponents(jax.random.fold_in(arg_keys[7], 71), 0),
        "norm_gain": jnp.clip(1.0 + 0.18 * jax.random.normal(arg_keys[2], (D,), jnp.float32), 0.099609375, 1.8984375).astype(jnp.bfloat16),
        "gate_weight": centred(arg_keys[3], (D, FF), D ** -0.5, 0.09375, ((0, 16), (1, 32))),
        "up_weight": centred(arg_keys[4], (D, FF), D ** -0.5, 0.09375, ((0, 16), (1, 32))),
        "down_weight": centred(arg_keys[5], (FF, D), FF ** -0.5, 0.046875, ((0, 32), (1, 16))),
        "cotangent": centred(arg_keys[6], (TOKENS, D), 1.0, 6.0, ((0, 32), (1, 16))),
    }


epsilon = 1e-05

def power_of_two(exponents):
    scales = jnp.zeros(exponents.shape, jnp.float32)
    for power_level in range(-2, 4):
        scales = scales + jnp.where(exponents == power_level, 2.0 ** power_level, 0.0).astype(jnp.float32)
    return scales

def sum_over_blocks(left_list, right_list, pieces):
    row_total = left_list[0].shape[0]
    out_cols = right_list[0].shape[1]
    inner = left_list[0].shape[1] // pieces
    lefts_split = tuple((item.reshape(row_total, pieces, inner).transpose(1, 0, 2) for item in left_list))
    rights_split = tuple((item.reshape(pieces, inner, out_cols) for item in right_list))

    def add_block(running, operands):
        left_blocks, right_blocks = operands
        partial_value = jnp.zeros((row_total, out_cols), jnp.float32)
        for left_block, right_block in zip(left_blocks, right_blocks):
            partial_value = partial_value + jnp.dot(left_block, right_block, preferred_element_type=jnp.float32)
        rounded = lax.optimization_barrier(partial_value.astype(jnp.bfloat16))
        return (running + rounded.astype(jnp.float32), None)
    running, _ = lax.scan(add_block, jnp.zeros((row_total, out_cols), jnp.float32), (lefts_split, rights_split))
    return running

def reference(mantissa, block_exponents, norm_gain, gate_weight, up_weight, down_weight, cotangent):
    expanded = jnp.repeat(block_exponents, BLOCK, axis=1)
    values = mantissa.astype(jnp.float32) * power_of_two(expanded)
    mean_square = lax.optimization_barrier(jnp.mean(values * values, axis=1, keepdims=True))
    normed = (values * lax.rsqrt(mean_square + epsilon) * norm_gain.astype(jnp.float32)).astype(jnp.bfloat16)
    gate_value = sum_over_blocks((normed,), (gate_weight,), N_DP)
    up_value = sum_over_blocks((normed,), (up_weight,), N_DP)
    logistic = jax.nn.sigmoid(gate_value)
    hidden = (gate_value * logistic * up_value).astype(jnp.bfloat16)
    mlp_output = sum_over_blocks((hidden,), (down_weight,), N_TENSOR).astype(jnp.bfloat16)
    back_sum = sum_over_blocks((cotangent,), (down_weight.T,), N_DP)
    dgate = (back_sum * up_value * logistic * (1.0 + gate_value * (1.0 - logistic))).astype(jnp.bfloat16)
    dup_value = (back_sum * gate_value * logistic).astype(jnp.bfloat16)
    input_grad = sum_over_blocks((dgate, dup_value), (gate_weight.T, up_weight.T), N_TENSOR).astype(jnp.bfloat16)
    grad_gate = jnp.dot(normed.T, dgate, preferred_element_type=jnp.float32)
    grad_up = jnp.dot(normed.T, dup_value, preferred_element_type=jnp.float32)
    grad_down = jnp.dot(hidden.T, cotangent, preferred_element_type=jnp.float32)
    return (mlp_output, input_grad, grad_gate, grad_up, grad_down)
```

```python
import jax
import jax.numpy as jnp
from jax import lax
from jax.experimental import pallas as pl
from jax.experimental.pallas import tpu as pltpu
from jax.sharding import PartitionSpec as P

BLOCK = 16
EPSILON = 1e-05
FULL_WIDTH = 4096
MESH = pl.DeviceIdType.MESH
F32, BF16 = jnp.float32, jnp.bfloat16

NX, NY, NZ = 4, 4, 16
HID = 448
WID = 256
COLS = 1408
BACK = 2 * HID
SPANS = ((0, 640), (640, 1408))

CHUNKS = ((0, 1, -1, 2), (-2, 3, -3, 4), (-4, 5, -5, 6), (-6, 7, -7, 8))
SLOT = {d: (k, p) for k, ds in enumerate(CHUNKS) for p, d in enumerate(ds)}
DIRECT = (5,)
SCHEDULE = (
    "X-1 X1 X-2 X2",
    "A0 X3 X-3 X-4",
    "X4 A1 X5 X-5",
    "B000 B001 B010 B011",
    "X6 X-6 B100 B101",
    "B110 B111 A2 X7",
    "X-7 C01 C00 X8",
    "C10 C11 A3 B200",
    "B201 B210 B211 D0",
    "D1 B300 B301 B310",
    "B311 C21 C20 E00",
    "E01 E11 E10 C30",
    "C31 D2 F000 F001",
    "F010 F011 F100 F101",
    "F110 F111 D3 E20",
    "E21 G0 R0 G1",
    "R1 I0 E30 F200",
    "F201 F210 F211 I1",
    "E31 F300 F301 J3",
    "F310 F311 G2 R2",
    "I2 G3 J1 R3",
    "I3 J-7 J-3 J7",
    "J-5 J-1 J5",
)


def dot(a, b, dims):
    return lax.dot_general(a, b, (dims, ((), ())), preferred_element_type=F32)


def rounded(total):
    tail = total[:, -128:]
    lane = lax.broadcasted_iota(jnp.int32, tail.shape, 1)
    lost = pltpu.roll(tail - tail.astype(BF16).astype(F32), 1, 1)
    tail = tail + jnp.where(lane == 65, lost, 0.0)
    return jnp.concatenate([total[:, :-128], tail], axis=1).astype(BF16)


def layer(
    m_hbm, e_hbm, g_ref, wg_hbm, wu_hbm, wd_hbm, c_hbm,
    acts_ref, joined_ref, down_ref,
    MV, EV, X, WJ, WD, PB, R1A, R1B, R2A, R2B, H, Q, E, S, LAND, ss, rs, ls,
):
    dp, tn = lax.axis_index("dp"), lax.axis_index("tensor")
    x, y = dp // NY, lax.rem(dp, NY)
    z, core = tn // 2, lax.rem(tn, 2)
    R1, R2 = (R1A, R1B), (R2A, R2B)

    def at(dx=0, dy=0, dz=0, dc=0):
        px, py = lax.rem(x + dx + NX, NX), lax.rem(y + dy + NY, NY)
        pz, pc = lax.rem(z + dz + NZ, NZ), lax.rem(core + dc, 2)
        return (px * NY + py, pz * 2 + pc)

    def on(axis, d):
        return at(dx=d) if axis == "x" else at(dy=d)

    counter = [0]
    pending = []

    def send(src, dst, device):
        n = counter[0]
        counter[0] += 1
        copy = pltpu.make_async_remote_copy(
            src_ref=src, dst_ref=dst, send_sem=ss.at[n], recv_sem=rs.at[n], device_id=device, device_id_type=MESH
        )
        copy.start()
        pending.append(copy)
        return copy

    barrier = pltpu.get_barrier_semaphore()
    near = [at(dc=1)] + [at(dz=d) for d in (1, 2, -1, -2)]
    near += [at(dx=d) for d in (1, 2, 3)] + [at(dy=d) for d in (1, 2, 3)]
    for device in near:
        pl.semaphore_signal(barrier, inc=1, device_id=device, device_id_type=MESH)

    own = X.at[SLOT[0][0], SLOT[0][1], 0]
    fetch = [
        pltpu.make_async_copy(src, dst, ls.at[i])
        for i, (src, dst) in enumerate((
            (m_hbm, MV),
            (e_hbm, EV),
            (c_hbm, own.at[:, pl.ds(WID, WID)]),
            (wg_hbm, WJ.at[pl.ds(0, HID)]),
            (wu_hbm, WJ.at[pl.ds(HID, HID)]),
            (wd_hbm, WD.at[pl.ds(0, HID)]),
        ))
    ]
    for copy in fetch:
        copy.start()
    row = lax.broadcasted_iota(jnp.int32, (WID, WID), 0)
    col = lax.broadcasted_iota(jnp.int32, (WID, WID), 1)
    pick = jnp.where(row == dp * (WID // BLOCK) + col // BLOCK, 1.0, 0.0).astype(BF16)
    WD[HID:] = jnp.zeros((64, WID), BF16)

    for copy in fetch[:3]:
        copy.wait()
    exponents = EV[...]
    scales = jnp.zeros(exponents.shape, F32)
    for level in range(-2, 4):
        scales = scales + jnp.where(exponents == level, 2.0**level, 0.0)
    scales = dot(scales.astype(BF16), pick, ((1,), (0,)))
    own[:, :WID] = (MV[...].astype(F32) * scales).astype(BF16)

    pl.semaphore_wait(barrier, len(near))

    ring = {}
    twin = {}

    def xat(d, who):
        return X.at[SLOT[d][0], SLOT[d][1], who]

    def f_pass(d):
        if d != 0:
            ring[d].wait_recv()
        for step in (-1, 1, -2, 2) if d == 0 else (-2,) if d < 0 else (2,):
            if -8 < d + step < 9:
                ring[d + step] = send(xat(d, 0), xat(d + step, 0), at(dz=-step))
        twin[d] = send(xat(d, 0), xat(d, 1), at(dc=1))

    def gain():
        return g_ref[...].astype(F32).reshape(1, WID)

    first, direct, second, gather2, gather1, forward = {}, {}, {}, {}, {}, {}
    swap, even, odd, last = {}, {}, {}, []

    def axes(k, h):
        return ("x", "y", x, y) if (k + h) % 2 == 0 else ("y", "x", y, x)

    def columns(h):
        return slice(*SPANS[h])

    def spot(k, h, index, half):
        two = pl.ds(2 * half, 2)
        return (k, index, two) if axes(k, h)[0] == "x" else (k, two, index)

    def piece(ref, k, h, index, half):
        a, b, c = spot(k, h, index, half)
        return ref.at[a, b, c, :, pl.ds(SPANS[h][0], SPANS[h][1] - SPANS[h][0])]

    def f_partial(k):
        for d in CHUNKS[k]:
            twin[d].wait_recv()
        both = X[k].reshape(256, 2 * WID)
        values = both[:, :WID].astype(F32)
        squares = jnp.sum(values * values, axis=1, keepdims=True)
        scaled = (values * gain()).astype(BF16)
        joined = dot(scaled, WJ[...], ((1,), (1,)))
        PB[k, :, :, :, :BACK] = joined.astype(BF16).reshape(4, 4, 16, BACK)
        back = dot(both[:, WID:], WD[...], ((1,), (1,)))
        lane = lax.broadcasted_iota(jnp.int32, back.shape, 1)
        high = squares.astype(BF16).astype(F32)
        back = jnp.where(lane == HID, high, jnp.where(lane == HID + 1, squares - high, back))
        PB[k, :, :, :, BACK:] = back.astype(BF16).reshape(4, 4, 16, 512)
        for h in range(2):
            a, b, ia, ib = axes(k, h)
            far = lax.rem(ia + 2, 4)
            first[k, h] = (
                send(piece(PB, k, h, far, 0), R1[h].at[k, 0], on(a, 1)),
                send(piece(PB, k, h, far, 1), R1[h].at[k, 1], on(a, -1)),
            )
        for h in range(2):
            a, b, ia, ib = axes(k, h)
            right, left = lax.rem(ia + 1, 4), lax.rem(ia + 3, 4)
            direct[k, h] = [
                send(piece(PB, k, h, right, 1), R1[h].at[k, 2], on(a, 1)),
                send(piece(PB, k, h, left, 0), R1[h].at[k, 3], on(a, -1)),
            ]

    def add_up(k, h, index, half, parts):
        a, b, c = spot(k, h, index, half)
        width = SPANS[h][1] - SPANS[h][0]
        total = PB[a, b, c, :, columns(h)].astype(F32)
        for part in parts:
            total = total + R1[h][k, part].astype(F32)
        total = total.reshape(32, width)
        total = rounded(total) if h == 1 else total.astype(BF16)
        PB[a, b, c, :, columns(h)] = total.reshape(2, 16, width)

    def f_merge(k, h, side):
        a, b, ia, ib = axes(k, h)
        to = lax.rem(ia + (1, 3)[side], 4)
        first[k, h][side].wait_recv()
        add_up(k, h, to, side, (side,))
        direct[k, h].append(send(piece(PB, k, h, to, side), R1[h].at[k, 4 + side], on(a, (1, -1)[side])))

    def f_second(k, h):
        a, b, ia, ib = axes(k, h)
        for copy in direct[k, h]:
            copy.wait_recv()
        add_up(k, h, ia, 0, (4, 3))
        add_up(k, h, ia, 1, (2, 5))
        second[k, h] = []
        for d in (2, 1, 3):
            to = lax.rem(ib + d, 4)
            px, py = (ia, to) if a == "x" else (to, ia)
            src = PB.at[k, px, py, :, pl.ds(SPANS[h][0], SPANS[h][1] - SPANS[h][0])]
            second[k, h].append(send(src, R2[h].at[k, d - 1], on(b, d)))

    def f_act(k):
        halves = []
        for h in range(2):
            for copy in second[k, h]:
                copy.wait_recv()
            total = PB[k, x, y, :, columns(h)].astype(F32)
            for part in range(3):
                total = total + R2[h][k, part].astype(F32)
            halves.append(total)
        total = jnp.concatenate(halves, axis=1)
        squares = total[:, 3 * HID : 3 * HID + 1] + total[:, 3 * HID + 1 : 3 * HID + 2]
        inv = lax.rsqrt(squares / FULL_WIDTH + EPSILON)
        gate = total[:, :HID] * inv
        up = total[:, HID : 2 * HID] * inv
        back = total[:, BACK : BACK + HID]
        sig = jax.nn.sigmoid(gate)
        hidden = gate * sig * up
        dgate = back * up * sig * (1.0 + gate * (1.0 - sig))
        dup = back * gate * sig
        high = inv.astype(BF16).astype(F32)
        lane = lax.broadcasted_iota(jnp.int32, (16, 64), 1)
        tail = jnp.where(lane == 0, high, jnp.where(lane == 1, inv - high, 0.0))
        H[k, x, y] = jnp.concatenate([dgate, dup, hidden, tail], axis=1).astype(BF16)
        for h in range(2):
            gather2[k, h] = []
        for d in (2, 1, 3):
            for h in range(2):
                b = axes(k, h)[1]
                mine = H.at[k, x, y, :, pl.ds(SPANS[h][0], SPANS[h][1] - SPANS[h][0])]
                gather2[k, h].append(send(mine, mine, on(b, d)))

    def f_gather(k, h):
        a, b, ia, ib = axes(k, h)
        for copy in gather2[k, h]:
            copy.wait_recv()
        low, top = piece(H, k, h, ia, 0), piece(H, k, h, ia, 1)
        gather1[k, h] = (send(low, low, on(a, 1)), send(top, top, on(a, -1)))
        forward[k, h] = [send(top, top, on(a, 1)), send(low, low, on(a, -1))]

    def f_forward(k, h, side):
        a, b, ia, ib = axes(k, h)
        gather1[k, h][side].wait_recv()
        block = piece(H, k, h, lax.rem(ia + (3, 1)[side], 4), side)
        forward[k, h].append(send(block, block, on(a, (1, -1)[side])))

    def f_project(k):
        for h in range(2):
            for copy in forward[k, h]:
                copy.wait_recv()
        full = H[k].reshape(256, COLS)
        mlp = dot(full[:, BACK:], WD[...], ((1,), (0,))).astype(BF16)
        grad = dot(full[:, :BACK], WJ[...], ((1,), (0,))).astype(BF16)
        for who in (1, 0):
            for p in range(4):
                at_row = 64 * p + 32 * who
                Q[k, who, p, :, :WID] = mlp[at_row : at_row + 32]
                Q[k, who, p, :, WID:] = grad[at_row : at_row + 32]
        swap[k] = send(Q.at[k, 1], E.at[k], at(dc=1))

    landings = []

    def hand_on(d, to, sign):
        n = len(landings)
        landings.append(d)
        k, p = SLOT[d]
        return n, send(S.at[k, p], LAND.at[n], at(dz=d - to))

    def f_pair(k):
        swap[k].wait_recv()
        S[k] = (Q[k, 0].astype(F32) + E[k].astype(F32)).astype(BF16)
        for d in CHUNKS[k]:
            sign = 1 if d > 0 else -1
            if abs(d) == 2:
                last.append(hand_on(d, 0, sign))
            elif d and d % 2 == 0:
                even[d] = hand_on(d, d - sign, sign)

    def f_odd(d):
        k, p = SLOT[d]
        sign = 1 if d > 0 else -1
        total = S[k, p].astype(F32)
        for table, other in ((even, d + sign), (odd, d + 2 * sign)):
            if other in table:
                n, copy = table[other]
                copy.wait_recv()
                total = total + LAND[n].astype(F32)
        S[k, p] = total.astype(BF16)
        if abs(d) == 1 or abs(d) in DIRECT:
            last.append(hand_on(d, 0, sign))
        else:
            odd[d] = hand_on(d, d - 2 * sign, sign)

    started = []

    def f_grads(k):
        full = H[k].reshape(256, COLS)
        both = X[k].reshape(256, 2 * WID)
        inv = full[:, 3 * HID : 3 * HID + 1].astype(F32) + full[:, 3 * HID + 1 : 3 * HID + 2].astype(F32)
        normed = (both[:, :WID].astype(F32) * inv * gain()).astype(BF16)
        joined = dot(full[:, :BACK], normed, ((0,), (0,)))
        down = dot(full[:, BACK:], both[:, WID:], ((0,), (0,)))[:HID]
        if started:
            joined_ref[...] += joined
            down_ref[...] += down
        else:
            joined_ref[...] = joined
            down_ref[...] = down
        started.append(k)

    steps = {
        "X": f_pass, "A": f_partial, "B": f_merge, "C": f_second, "D": f_act, "E": f_gather, "F": f_forward,
        "G": f_project, "I": f_pair, "J": f_odd, "R": f_grads,
    }
    f_pass(0)
    for copy in fetch[3:]:
        copy.wait()
    for line in SCHEDULE:
        for step in line.split():
            numbers = (int(step[1:]),) if step[0] in "XJ" else tuple(int(c) for c in step[1:])
            steps[step[0]](*numbers)

    k, p = SLOT[0]
    total = S[k, p].astype(F32)
    for n, copy in last:
        copy.wait_recv()
        total = total + LAND[n].astype(F32)
    acts_ref[...] = total.astype(BF16)
    for copy in pending:
        copy.wait_send()


def deliver(acts, joined, down, out_ref, ig_ref, gg_ref, gu_ref, gd_ref, sems):
    copies = [
        pltpu.make_async_copy(src, dst, sems.at[i])
        for i, (src, dst) in enumerate((
            (joined.at[pl.ds(0, HID)], gg_ref),
            (joined.at[pl.ds(HID, HID)], gu_ref),
            (down, gd_ref),
            (acts.at[:, pl.ds(0, WID)], out_ref),
            (acts.at[:, pl.ds(WID, WID)], ig_ref),
        ))
    ]
    for copy in copies:
        copy.start()
    for copy in copies:
        copy.wait()


COPIES = 15 + 16 + 36 * 4 + 4 + 15


def shards(mantissa, block_exponents, norm_gain, gate_weight, up_weight, down_weight, cotangent):
    vmem = pl.BlockSpec(memory_space=pltpu.VMEM)
    hbm = pl.BlockSpec(memory_space=pltpu.HBM)
    widths = [b - a for a, b in SPANS]
    acts, joined, down = pl.pallas_call(
        layer,
        out_shape=(
            jax.ShapeDtypeStruct((32, 2 * WID), BF16),
            jax.ShapeDtypeStruct((BACK, WID), F32),
            jax.ShapeDtypeStruct((HID, WID), F32),
        ),
        in_specs=[hbm, hbm, vmem, hbm, hbm, hbm, hbm],
        out_specs=[vmem] * 3,
        scratch_shapes=[
            pltpu.VMEM((32, WID), BF16),
            pltpu.VMEM((32, WID), jnp.int32),
            pltpu.VMEM((4, 4, 2, 32, 2 * WID), BF16),
            pltpu.VMEM((BACK, WID), BF16),
            pltpu.VMEM((512, WID), BF16),
            pltpu.VMEM((4, 4, 4, 16, COLS), BF16),
            pltpu.VMEM((4, 6, 2, 16, widths[0]), BF16),
            pltpu.VMEM((4, 6, 2, 16, widths[1]), BF16),
            pltpu.VMEM((4, 3, 16, widths[0]), BF16),
            pltpu.VMEM((4, 3, 16, widths[1]), BF16),
            pltpu.VMEM((4, 4, 4, 16, COLS), BF16),
            pltpu.VMEM((4, 2, 4, 32, 2 * WID), BF16),
            pltpu.VMEM((4, 4, 32, 2 * WID), BF16),
            pltpu.VMEM((4, 4, 32, 2 * WID), BF16),
            pltpu.VMEM((15, 32, 2 * WID), BF16),
            pltpu.SemaphoreType.DMA((COPIES,)),
            pltpu.SemaphoreType.DMA((COPIES,)),
            pltpu.SemaphoreType.DMA((6,)),
        ],
        compiler_params=pltpu.CompilerParams(collective_id=0, has_side_effects=True, vmem_limit_bytes=48 << 20),
        name="swiglu_layer",
    )(mantissa, block_exponents, norm_gain, gate_weight.T, up_weight.T, down_weight, cotangent)
    out, grad, gg, gu, gd = pl.pallas_call(
        deliver,
        out_shape=(
            jax.ShapeDtypeStruct((32, WID), BF16),
            jax.ShapeDtypeStruct((32, WID), BF16),
            jax.ShapeDtypeStruct((HID, WID), F32),
            jax.ShapeDtypeStruct((HID, WID), F32),
            jax.ShapeDtypeStruct((HID, WID), F32),
        ),
        in_specs=[vmem] * 3,
        out_specs=[hbm] * 5,
        scratch_shapes=[pltpu.SemaphoreType.DMA((5,))],
        compiler_params=pltpu.CompilerParams(vmem_limit_bytes=2 << 20),
        name="deliver",
    )(acts, joined, down)
    return out, grad, gg.T, gu.T, gd


def solution(mesh):
    in_specs = (
        P("tensor", "dp"),
        P("tensor", None),
        P("dp"),
        P("dp", "tensor"),
        P("dp", "tensor"),
        P("tensor", "dp"),
        P("tensor", "dp"),
    )
    out_specs = (
        P("tensor", "dp"),
        P("tensor", "dp"),
        P("dp", "tensor"),
        P("dp", "tensor"),
        P("tensor", "dp"),
    )
    return jax.shard_map(shards, mesh=mesh, in_specs=in_specs, out_specs=out_specs, check_vma=False)
```

```python
import jax
import jax.numpy as jnp
from jax import lax
from jax.experimental import pallas as pl
from jax.experimental.pallas import tpu as pltpu
from jax.sharding import PartitionSpec as P

BLOCK = 16
EPSILON = 1e-05
FULL_WIDTH = 4096
MESH = pl.DeviceIdType.MESH
F32, BF16 = jnp.float32, jnp.bfloat16

NX, NY, NZ = 4, 4, 16
HID = 448
WID = 256
COLS = 1408
BACK = 2 * HID
SPANS = ((0, 640), (640, 1408))

CHUNKS = ((0, 1, -1, 2), (-2, 3, -3, 4), (-4, 5, -5, 6), (-6, 7, -7, 8))
SLOT = {d: (k, p) for k, ds in enumerate(CHUNKS) for p, d in enumerate(ds)}
DIRECT = (5,)
SCHEDULE = (
    "X-1 X1 X-2 X2",
    "A0 X-3 X3 X-4",
    "X4 B000 B001 B010",
    "B011 A1 X-5 X5",
    "X-6 C00 X6 C01",
    "B110 B111 B100 B101",
    "A2 X-7 X7 X8",
    "D0 C10 C11 A3",
    "B210 B211 B200 B201",
    "E00 E01 D1 B300",
    "B301 B310 B311 C21",
    "C20 F010 F011 F000",
    "F001 E10 E11 C31",
    "C30 D2 G0 R0",
    "F100 F101 F110 F111",
    "I0 D3 E20 E21",
    "G1 R1 I1 E30",
    "E31 F200 F201 F210",
    "F211 J3 F300 F301",
    "F310 F311 G2 R2",
    "J1 G3 R3 I2",
    "I3 J-7 J-3 J7",
    "J-5 J-1 J5",
)


def dot(a, b, dims):
    return lax.dot_general(a, b, (dims, ((), ())), preferred_element_type=F32)


def rounded(total):
    tail = total[:, -128:]
    lane = lax.broadcasted_iota(jnp.int32, tail.shape, 1)
    lost = pltpu.roll(tail - tail.astype(BF16).astype(F32), 1, 1)
    tail = tail + jnp.where(lane == 65, lost, 0.0)
    return jnp.concatenate([total[:, :-128], tail], axis=1).astype(BF16)


def layer(
    m_hbm, e_hbm, g_ref, wg_hbm, wu_hbm, wd_hbm, c_hbm,
    acts_hbm, joined_hbm, down_hbm,
    MV, EV, X, WJ, WD, PB, R1A, R1B, R2A, R2B, H, Q, E, S, LAND, joined_ref, down_ref, acts_ref, ss, rs, ls, ws,
):
    dp, tn = lax.axis_index("dp"), lax.axis_index("tensor")
    x, y = dp // NY, lax.rem(dp, NY)
    z, core = tn // 2, lax.rem(tn, 2)
    R1, R2 = (R1A, R1B), (R2A, R2B)

    def at(dx=0, dy=0, dz=0, dc=0):
        px, py = lax.rem(x + dx + NX, NX), lax.rem(y + dy + NY, NY)
        pz, pc = lax.rem(z + dz + NZ, NZ), lax.rem(core + dc, 2)
        return (px * NY + py, pz * 2 + pc)

    def on(axis, d):
        return at(dx=d) if axis == "x" else at(dy=d)

    counter = [0]
    pending = []

    def send(src, dst, device):
        n = counter[0]
        counter[0] += 1
        copy = pltpu.make_async_remote_copy(
            src_ref=src, dst_ref=dst, send_sem=ss.at[n], recv_sem=rs.at[n], device_id=device, device_id_type=MESH
        )
        copy.start()
        pending.append(copy)
        return copy

    barrier = pltpu.get_barrier_semaphore()
    near = [at(dc=1)] + [at(dz=d) for d in (1, 2, -1, -2)]
    near += [at(dx=d) for d in (1, 2, 3)] + [at(dy=d) for d in (1, 2, 3)]
    for device in near:
        pl.semaphore_signal(barrier, inc=1, device_id=device, device_id_type=MESH)

    own = X.at[SLOT[0][0], SLOT[0][1], 0]
    fetch = [
        pltpu.make_async_copy(src, dst, ls.at[i])
        for i, (src, dst) in enumerate((
            (m_hbm, MV),
            (e_hbm, EV),
            (c_hbm, own.at[:, pl.ds(WID, WID)]),
            (wg_hbm, WJ.at[pl.ds(0, HID)]),
            (wu_hbm, WJ.at[pl.ds(HID, HID)]),
            (wd_hbm, WD.at[pl.ds(0, HID)]),
        ))
    ]
    for copy in fetch:
        copy.start()
    row = lax.broadcasted_iota(jnp.int32, (WID, WID), 0)
    col = lax.broadcasted_iota(jnp.int32, (WID, WID), 1)
    pick = jnp.where(row == dp * (WID // BLOCK) + col // BLOCK, 1.0, 0.0).astype(BF16)
    WD[HID:] = jnp.zeros((64, WID), BF16)

    for copy in fetch[:3]:
        copy.wait()
    exponents = EV[...]
    scales = jnp.zeros(exponents.shape, F32)
    for level in range(-2, 4):
        scales = scales + jnp.where(exponents == level, 2.0**level, 0.0)
    scales = dot(scales.astype(BF16), pick, ((1,), (0,)))
    own[:, :WID] = (MV[...].astype(F32) * scales).astype(BF16)

    pl.semaphore_wait(barrier, len(near))

    ring = {}
    twin = {}

    def xat(d, who):
        return X.at[SLOT[d][0], SLOT[d][1], who]

    def f_pass(d):
        if d != 0:
            ring[d].wait_recv()
        for step in (-1, 1, -2, 2) if d == 0 else (-2,) if d < 0 else (2,):
            if -8 < d + step < 9:
                ring[d + step] = send(xat(d, 0), xat(d + step, 0), at(dz=-step))
        twin[d] = send(xat(d, 0), xat(d, 1), at(dc=1))

    def gain():
        return g_ref[...].astype(F32).reshape(1, WID)

    first, direct, second, gather2, gather1, forward = {}, {}, {}, {}, {}, {}
    swap, even, odd, last = {}, {}, {}, []

    def axes(k, h):
        return ("x", "y", x, y) if (k + h) % 2 == 0 else ("y", "x", y, x)

    def columns(h):
        return slice(*SPANS[h])

    def spot(k, h, index, half):
        two = pl.ds(2 * half, 2)
        return (k, index, two) if axes(k, h)[0] == "x" else (k, two, index)

    def piece(ref, k, h, index, half):
        a, b, c = spot(k, h, index, half)
        return ref.at[a, b, c, :, pl.ds(SPANS[h][0], SPANS[h][1] - SPANS[h][0])]

    def f_partial(k):
        for d in CHUNKS[k]:
            twin[d].wait_recv()
        both = X[k].reshape(256, 2 * WID)
        values = both[:, :WID].astype(F32)
        squares = jnp.sum(values * values, axis=1, keepdims=True)
        scaled = (values * gain()).astype(BF16)
        joined = dot(scaled, WJ[...], ((1,), (1,)))
        PB[k, :, :, :, :BACK] = joined.astype(BF16).reshape(4, 4, 16, BACK)
        back = dot(both[:, WID:], WD[...], ((1,), (1,)))
        lane = lax.broadcasted_iota(jnp.int32, back.shape, 1)
        high = squares.astype(BF16).astype(F32)
        back = jnp.where(lane == HID, high, jnp.where(lane == HID + 1, squares - high, back))
        PB[k, :, :, :, BACK:] = back.astype(BF16).reshape(4, 4, 16, 512)
        for h in range(2):
            a, b, ia, ib = axes(k, h)
            far = lax.rem(ia + 2, 4)
            first[k, h] = (
                send(piece(PB, k, h, far, 0), R1[h].at[k, 0], on(a, 1)),
                send(piece(PB, k, h, far, 1), R1[h].at[k, 1], on(a, -1)),
            )
        for h in range(2):
            a, b, ia, ib = axes(k, h)
            right, left = lax.rem(ia + 1, 4), lax.rem(ia + 3, 4)
            direct[k, h] = [
                send(piece(PB, k, h, right, 1), R1[h].at[k, 2], on(a, 1)),
                send(piece(PB, k, h, left, 0), R1[h].at[k, 3], on(a, -1)),
            ]

    def add_up(k, h, index, half, parts):
        a, b, c = spot(k, h, index, half)
        width = SPANS[h][1] - SPANS[h][0]
        total = PB[a, b, c, :, columns(h)].astype(F32)
        for part in parts:
            total = total + R1[h][k, part].astype(F32)
        total = total.reshape(32, width)
        total = rounded(total) if h == 1 else total.astype(BF16)
        PB[a, b, c, :, columns(h)] = total.reshape(2, 16, width)

    def f_merge(k, h, side):
        a, b, ia, ib = axes(k, h)
        to = lax.rem(ia + (1, 3)[side], 4)
        first[k, h][side].wait_recv()
        add_up(k, h, to, side, (side,))
        direct[k, h].append(send(piece(PB, k, h, to, side), R1[h].at[k, 4 + side], on(a, (1, -1)[side])))

    def f_second(k, h):
        a, b, ia, ib = axes(k, h)
        for copy in direct[k, h]:
            copy.wait_recv()
        add_up(k, h, ia, 0, (4, 3))
        add_up(k, h, ia, 1, (2, 5))
        second[k, h] = []
        for d in (2, 1, 3):
            to = lax.rem(ib + d, 4)
            px, py = (ia, to) if a == "x" else (to, ia)
            src = PB.at[k, px, py, :, pl.ds(SPANS[h][0], SPANS[h][1] - SPANS[h][0])]
            second[k, h].append(send(src, R2[h].at[k, d - 1], on(b, d)))

    def f_act(k):
        halves = []
        for h in range(2):
            for copy in second[k, h]:
                copy.wait_recv()
            total = PB[k, x, y, :, columns(h)].astype(F32)
            for part in range(3):
                total = total + R2[h][k, part].astype(F32)
            halves.append(total)
        total = jnp.concatenate(halves, axis=1)
        squares = total[:, 3 * HID : 3 * HID + 1] + total[:, 3 * HID + 1 : 3 * HID + 2]
        inv = lax.rsqrt(squares / FULL_WIDTH + EPSILON)
        gate = total[:, :HID] * inv
        up = total[:, HID : 2 * HID] * inv
        back = total[:, BACK : BACK + HID]
        sig = jax.nn.sigmoid(gate)
        hidden = gate * sig * up
        dgate = back * up * sig * (1.0 + gate * (1.0 - sig))
        dup = back * gate * sig
        high = inv.astype(BF16).astype(F32)
        lane = lax.broadcasted_iota(jnp.int32, (16, 64), 1)
        tail = jnp.where(lane == 0, high, jnp.where(lane == 1, inv - high, 0.0))
        H[k, x, y] = jnp.concatenate([dgate, dup, hidden, tail], axis=1).astype(BF16)
        for h in range(2):
            gather2[k, h] = []
        for d in (2, 1, 3):
            for h in range(2):
                b = axes(k, h)[1]
                mine = H.at[k, x, y, :, pl.ds(SPANS[h][0], SPANS[h][1] - SPANS[h][0])]
                gather2[k, h].append(send(mine, mine, on(b, d)))

    def f_gather(k, h):
        a, b, ia, ib = axes(k, h)
        for copy in gather2[k, h]:
            copy.wait_recv()
        low, top = piece(H, k, h, ia, 0), piece(H, k, h, ia, 1)
        gather1[k, h] = (send(low, low, on(a, 1)), send(top, top, on(a, -1)))
        forward[k, h] = [send(top, top, on(a, 1)), send(low, low, on(a, -1))]

    def f_forward(k, h, side):
        a, b, ia, ib = axes(k, h)
        gather1[k, h][side].wait_recv()
        block = piece(H, k, h, lax.rem(ia + (3, 1)[side], 4), side)
        forward[k, h].append(send(block, block, on(a, (1, -1)[side])))

    def f_project(k):
        for h in range(2):
            for copy in forward[k, h]:
                copy.wait_recv()
        full = H[k].reshape(256, COLS)
        mlp = dot(full[:, BACK:], WD[...], ((1,), (0,))).astype(BF16)
        grad = dot(full[:, :BACK], WJ[...], ((1,), (0,))).astype(BF16)
        for who in (1, 0):
            for p in range(4):
                at_row = 64 * p + 32 * who
                Q[k, who, p, :, :WID] = mlp[at_row : at_row + 32]
                Q[k, who, p, :, WID:] = grad[at_row : at_row + 32]
        swap[k] = send(Q.at[k, 1], E.at[k], at(dc=1))

    landings = []

    def hand_on(d, to, sign):
        n = len(landings)
        landings.append(d)
        k, p = SLOT[d]
        return n, send(S.at[k, p], LAND.at[n], at(dz=d - to))

    def f_pair(k):
        swap[k].wait_recv()
        S[k] = (Q[k, 0].astype(F32) + E[k].astype(F32)).astype(BF16)
        for d in CHUNKS[k]:
            sign = 1 if d > 0 else -1
            if abs(d) == 2:
                last.append(hand_on(d, 0, sign))
            elif d and d % 2 == 0:
                even[d] = hand_on(d, d - sign, sign)

    def f_odd(d):
        k, p = SLOT[d]
        sign = 1 if d > 0 else -1
        total = S[k, p].astype(F32)
        for table, other in ((even, d + sign), (odd, d + 2 * sign)):
            if other in table:
                n, copy = table[other]
                copy.wait_recv()
                total = total + LAND[n].astype(F32)
        S[k, p] = total.astype(BF16)
        if abs(d) == 1 or abs(d) in DIRECT:
            last.append(hand_on(d, 0, sign))
        else:
            odd[d] = hand_on(d, d - 2 * sign, sign)

    started, results = [], []

    def f_grads(k):
        full = H[k].reshape(256, COLS)
        both = X[k].reshape(256, 2 * WID)
        inv = full[:, 3 * HID : 3 * HID + 1].astype(F32) + full[:, 3 * HID + 1 : 3 * HID + 2].astype(F32)
        normed = (both[:, :WID].astype(F32) * inv * gain()).astype(BF16)
        joined = dot(full[:, :BACK], normed, ((0,), (0,)))
        down = dot(full[:, BACK:], both[:, WID:], ((0,), (0,)))[:HID]
        if started:
            joined_ref[...] += joined
            down_ref[...] += down
        else:
            joined_ref[...] = joined
            down_ref[...] = down
        started.append(k)
        if len(started) == len(CHUNKS):
            results.append(pltpu.make_async_copy(joined_ref, joined_hbm, ws.at[0]))
            results.append(pltpu.make_async_copy(down_ref, down_hbm, ws.at[1]))
            for copy in results:
                copy.start()

    steps = {
        "X": f_pass, "A": f_partial, "B": f_merge, "C": f_second, "D": f_act, "E": f_gather, "F": f_forward,
        "G": f_project, "I": f_pair, "J": f_odd, "R": f_grads,
    }
    f_pass(0)
    for copy in fetch[3:]:
        copy.wait()
    for line in SCHEDULE:
        for step in line.split():
            numbers = (int(step[1:]),) if step[0] in "XJ" else tuple(int(c) for c in step[1:])
            steps[step[0]](*numbers)

    k, p = SLOT[0]
    total = S[k, p].astype(F32)
    for n, copy in last:
        copy.wait_recv()
        total = total + LAND[n].astype(F32)
    acts_ref[...] = total.astype(BF16)
    results.append(pltpu.make_async_copy(acts_ref, acts_hbm, ws.at[2]))
    results[-1].start()
    for copy in pending:
        copy.wait_send()
    for copy in results:
        copy.wait()


def deliver(acts, joined, down, out_ref, ig_ref, gg_ref, gu_ref, gd_ref, AV, JV, DV, rsem, wsem):
    half = HID // 2
    plan = [(acts, AV, (AV.at[:, pl.ds(0, WID)], out_ref), (AV.at[:, pl.ds(WID, WID)], ig_ref))]
    for src, via, start, dst in ((joined, JV, 0, gg_ref), (joined, JV, HID, gu_ref), (down, DV, 0, gd_ref)):
        for part in (0, half):
            there = pl.ds(start + part, half)
            plan.append((src.at[there], via.at[there], (via.at[there], dst.at[pl.ds(part, half)])))
    reads = [pltpu.make_async_copy(entry[0], entry[1], rsem.at[i]) for i, entry in enumerate(plan)]
    for copy in reads:
        copy.start()
    writes = []
    for copy, entry in zip(reads, plan):
        copy.wait()
        for src, dst in entry[2:]:
            writes.append(pltpu.make_async_copy(src, dst, wsem.at[len(writes)]))
            writes[-1].start()
    for copy in writes:
        copy.wait()


COPIES = 15 + 16 + 36 * 4 + 4 + 15


def shards(mantissa, block_exponents, norm_gain, gate_weight, up_weight, down_weight, cotangent):
    vmem = pl.BlockSpec(memory_space=pltpu.VMEM)
    hbm = pl.BlockSpec(memory_space=pltpu.HBM)
    widths = [b - a for a, b in SPANS]
    acts, joined, down = pl.pallas_call(
        layer,
        out_shape=(
            jax.ShapeDtypeStruct((32, 2 * WID), BF16),
            jax.ShapeDtypeStruct((BACK, WID), F32),
            jax.ShapeDtypeStruct((HID, WID), F32),
        ),
        in_specs=[hbm, hbm, vmem, hbm, hbm, hbm, hbm],
        out_specs=[hbm] * 3,
        scratch_shapes=[
            pltpu.VMEM((32, WID), BF16),
            pltpu.VMEM((32, WID), jnp.int32),
            pltpu.VMEM((4, 4, 2, 32, 2 * WID), BF16),
            pltpu.VMEM((BACK, WID), BF16),
            pltpu.VMEM((512, WID), BF16),
            pltpu.VMEM((4, 4, 4, 16, COLS), BF16),
            pltpu.VMEM((4, 6, 2, 16, widths[0]), BF16),
            pltpu.VMEM((4, 6, 2, 16, widths[1]), BF16),
            pltpu.VMEM((4, 3, 16, widths[0]), BF16),
            pltpu.VMEM((4, 3, 16, widths[1]), BF16),
            pltpu.VMEM((4, 4, 4, 16, COLS), BF16),
            pltpu.VMEM((4, 2, 4, 32, 2 * WID), BF16),
            pltpu.VMEM((4, 4, 32, 2 * WID), BF16),
            pltpu.VMEM((4, 4, 32, 2 * WID), BF16),
            pltpu.VMEM((15, 32, 2 * WID), BF16),
            pltpu.VMEM((BACK, WID), F32),
            pltpu.VMEM((HID, WID), F32),
            pltpu.VMEM((32, 2 * WID), BF16),
            pltpu.SemaphoreType.DMA((COPIES,)),
            pltpu.SemaphoreType.DMA((COPIES,)),
            pltpu.SemaphoreType.DMA((6,)),
            pltpu.SemaphoreType.DMA((3,)),
        ],
        compiler_params=pltpu.CompilerParams(collective_id=0, has_side_effects=True, vmem_limit_bytes=60 << 20),
        name="swiglu_layer",
    )(mantissa, block_exponents, norm_gain, gate_weight.T, up_weight.T, down_weight, cotangent)
    out, grad, gg, gu, gd = pl.pallas_call(
        deliver,
        out_shape=(
            jax.ShapeDtypeStruct((32, WID), BF16),
            jax.ShapeDtypeStruct((32, WID), BF16),
            jax.ShapeDtypeStruct((HID, WID), F32),
            jax.ShapeDtypeStruct((HID, WID), F32),
            jax.ShapeDtypeStruct((HID, WID), F32),
        ),
        in_specs=[hbm] * 3,
        out_specs=[hbm] * 5,
        scratch_shapes=[
            pltpu.VMEM((32, 2 * WID), BF16),
            pltpu.VMEM((BACK, WID), F32),
            pltpu.VMEM((HID, WID), F32),
            pltpu.SemaphoreType.DMA((7,)),
            pltpu.SemaphoreType.DMA((8,)),
        ],
        compiler_params=pltpu.CompilerParams(vmem_limit_bytes=60 << 20),
        name="deliver",
    )(acts, joined, down)
    return out, grad, gg.T, gu.T, gd


def solution(mesh):
    in_specs = (
        P("tensor", "dp"),
        P("tensor", None),
        P("dp"),
        P("dp", "tensor"),
        P("dp", "tensor"),
        P("tensor", "dp"),
        P("tensor", "dp"),
    )
    out_specs = (
        P("tensor", "dp"),
        P("tensor", "dp"),
        P("dp", "tensor"),
        P("dp", "tensor"),
        P("tensor", "dp"),
    )
    return jax.shard_map(shards, mesh=mesh, in_specs=in_specs, out_specs=out_specs, check_vma=False)
```

```python
import jax
import jax.numpy as jnp
from jax import lax
from jax.experimental import pallas as pl
from jax.experimental.pallas import tpu as pltpu
from jax.sharding import PartitionSpec as P

BLOCK = 16
EPSILON = 1e-05
FULL_WIDTH = 4096
MESH = pl.DeviceIdType.MESH
F32, BF16 = jnp.float32, jnp.bfloat16

NX, NY, NZ = 4, 4, 16
HID = 448
WID = 256
COLS = 1408
BACK = 2 * HID
SPANS = ((0, 640), (640, 1408))

CHUNKS = ((0, 1, -1, 2), (-2, 3, -3, 4), (-4, 5, -5, 6), (-6, 7, -7, 8))
SLOT = {d: (k, p) for k, ds in enumerate(CHUNKS) for p, d in enumerate(ds)}
DIRECT = (5,)
SCHEDULE = (
    "X-1 X1 X-2 X2",
    "A0 X-3 X3 X-4",
    "X4 B000 B001 A1",
    "B010 X5 X-5 B011",
    "X-6 X6 C00 B100",
    "B101 A2 X7 B110",
    "X-7 B111 C01 X8",
    "A3 C10 B200 B201",
    "B210 B211 C11 D0",
    "B300 B301 B310 B311",
    "C21 D1 C20 E00",
    "C30 E01 C31 E11",
    "D2 E10 F010 F011",
    "F000 F001 D3 F110",
    "F111 E20 F100 F101",
    "E21 G0 R0 E30",
    "E31 G1 I0 R1",
    "F200 F201 F210 F211",
    "I1 F310 F311 F300",
    "F301 G2 J3 R2",
    "G3 R3 I2 I3",
    "J-7 J1 J-3 J7",
    "J-5 J-1 J5",
)


def dot(a, b, dims):
    return lax.dot_general(a, b, (dims, ((), ())), preferred_element_type=F32)


def rounded(total):
    tail = total[:, -128:]
    lane = lax.broadcasted_iota(jnp.int32, tail.shape, 1)
    lost = pltpu.roll(tail - tail.astype(BF16).astype(F32), 1, 1)
    tail = tail + jnp.where(lane == 65, lost, 0.0)
    return jnp.concatenate([total[:, :-128], tail], axis=1).astype(BF16)


def layer(
    m_hbm, e_hbm, g_hbm, wg_hbm, wu_hbm, wd_hbm, c_hbm,
    acts_ref, joined_ref, down_ref,
    MV, EV, g_ref, X, WJ, WD, PB, R1A, R1B, R2A, R2B, H, Q, E, S, LAND, ss, rs, ls,
):
    dp, tn = lax.axis_index("dp"), lax.axis_index("tensor")
    x, y = dp // NY, lax.rem(dp, NY)
    z, core = tn // 2, lax.rem(tn, 2)
    R1, R2 = (R1A, R1B), (R2A, R2B)

    def at(dx=0, dy=0, dz=0, dc=0):
        px, py = lax.rem(x + dx + NX, NX), lax.rem(y + dy + NY, NY)
        pz, pc = lax.rem(z + dz + NZ, NZ), lax.rem(core + dc, 2)
        return (px * NY + py, pz * 2 + pc)

    def on(axis, d):
        return at(dx=d) if axis == "x" else at(dy=d)

    counter = [0]
    pending = []

    def send(src, dst, device):
        n = counter[0]
        counter[0] += 1
        copy = pltpu.make_async_remote_copy(
            src_ref=src, dst_ref=dst, send_sem=ss.at[n], recv_sem=rs.at[n], device_id=device, device_id_type=MESH
        )
        copy.start()
        pending.append(copy)
        return copy

    barrier = pltpu.get_barrier_semaphore()
    near = [at(dc=1)] + [at(dz=d) for d in (1, 2, -1, -2)]
    near += [at(dx=d) for d in (1, 2, 3)] + [at(dy=d) for d in (1, 2, 3)]
    for device in near:
        pl.semaphore_signal(barrier, inc=1, device_id=device, device_id_type=MESH)

    own = X.at[SLOT[0][0], SLOT[0][1], 0]
    fetch = [
        pltpu.make_async_copy(src, dst, ls.at[i])
        for i, (src, dst) in enumerate((
            (m_hbm, MV),
            (e_hbm, EV),
            (c_hbm, own.at[:, pl.ds(WID, WID)]),
            (wg_hbm, WJ.at[pl.ds(0, HID)]),
            (wu_hbm, WJ.at[pl.ds(HID, HID)]),
            (wd_hbm, WD.at[pl.ds(0, HID)]),
            (g_hbm, g_ref),
        ))
    ]
    for copy in fetch:
        copy.start()
    row = lax.broadcasted_iota(jnp.int32, (WID, WID), 0)
    col = lax.broadcasted_iota(jnp.int32, (WID, WID), 1)
    pick = jnp.where(row == dp * (WID // BLOCK) + col // BLOCK, 1.0, 0.0).astype(BF16)
    WD[HID:] = jnp.zeros((64, WID), BF16)

    for copy in fetch[:3]:
        copy.wait()
    exponents = EV[...]
    scales = jnp.zeros(exponents.shape, F32)
    for level in range(-2, 4):
        scales = scales + jnp.where(exponents == level, 2.0**level, 0.0)
    scales = dot(scales.astype(BF16), pick, ((1,), (0,)))
    own[:, :WID] = (MV[...].astype(F32) * scales).astype(BF16)

    pl.semaphore_wait(barrier, len(near))

    ring = {}
    twin = {}

    def xat(d, who):
        return X.at[SLOT[d][0], SLOT[d][1], who]

    def f_pass(d):
        if d != 0:
            ring[d].wait_recv()
        for step in (-1, 1, -2, 2) if d == 0 else (-2,) if d < 0 else (2,):
            if -8 < d + step < 9:
                ring[d + step] = send(xat(d, 0), xat(d + step, 0), at(dz=-step))
        twin[d] = send(xat(d, 0), xat(d, 1), at(dc=1))

    def gain():
        return g_ref[...].astype(F32).reshape(1, WID)

    first, direct, second, gather2, gather1, forward = {}, {}, {}, {}, {}, {}
    swap, even, odd, last = {}, {}, {}, []

    def axes(k, h):
        return ("x", "y", x, y) if (k + h) % 2 == 0 else ("y", "x", y, x)

    def columns(h):
        return slice(*SPANS[h])

    def spot(k, h, index, half):
        two = pl.ds(2 * half, 2)
        return (k, index, two) if axes(k, h)[0] == "x" else (k, two, index)

    def piece(ref, k, h, index, half):
        a, b, c = spot(k, h, index, half)
        return ref.at[a, b, c, :, pl.ds(SPANS[h][0], SPANS[h][1] - SPANS[h][0])]

    def f_partial(k):
        for d in CHUNKS[k]:
            twin[d].wait_recv()
        both = X[k].reshape(256, 2 * WID)
        values = both[:, :WID].astype(F32)
        squares = jnp.sum(values * values, axis=1, keepdims=True)
        scaled = (values * gain()).astype(BF16)
        joined = dot(scaled, WJ[...], ((1,), (1,)))
        PB[k, :, :, :, :BACK] = joined.astype(BF16).reshape(4, 4, 16, BACK)
        back = dot(both[:, WID:], WD[...], ((1,), (1,)))
        lane = lax.broadcasted_iota(jnp.int32, back.shape, 1)
        high = squares.astype(BF16).astype(F32)
        back = jnp.where(lane == HID, high, jnp.where(lane == HID + 1, squares - high, back))
        PB[k, :, :, :, BACK:] = back.astype(BF16).reshape(4, 4, 16, 512)
        for h in range(2):
            a, b, ia, ib = axes(k, h)
            far = lax.rem(ia + 2, 4)
            first[k, h] = (
                send(piece(PB, k, h, far, 0), R1[h].at[k, 0], on(a, 1)),
                send(piece(PB, k, h, far, 1), R1[h].at[k, 1], on(a, -1)),
            )
        for h in range(2):
            a, b, ia, ib = axes(k, h)
            right, left = lax.rem(ia + 1, 4), lax.rem(ia + 3, 4)
            direct[k, h] = [
                send(piece(PB, k, h, right, 1), R1[h].at[k, 2], on(a, 1)),
                send(piece(PB, k, h, left, 0), R1[h].at[k, 3], on(a, -1)),
            ]

    def add_up(k, h, index, half, parts):
        a, b, c = spot(k, h, index, half)
        width = SPANS[h][1] - SPANS[h][0]
        total = PB[a, b, c, :, columns(h)].astype(F32)
        for part in parts:
            total = total + R1[h][k, part].astype(F32)
        total = total.reshape(32, width)
        total = rounded(total) if h == 1 else total.astype(BF16)
        PB[a, b, c, :, columns(h)] = total.reshape(2, 16, width)

    def f_merge(k, h, side):
        a, b, ia, ib = axes(k, h)
        to = lax.rem(ia + (1, 3)[side], 4)
        first[k, h][side].wait_recv()
        add_up(k, h, to, side, (side,))
        direct[k, h].append(send(piece(PB, k, h, to, side), R1[h].at[k, 4 + side], on(a, (1, -1)[side])))

    def f_second(k, h):
        a, b, ia, ib = axes(k, h)
        for copy in direct[k, h]:
            copy.wait_recv()
        add_up(k, h, ia, 0, (4, 3))
        add_up(k, h, ia, 1, (2, 5))
        second[k, h] = []
        for d in (2, 1, 3):
            to = lax.rem(ib + d, 4)
            px, py = (ia, to) if a == "x" else (to, ia)
            src = PB.at[k, px, py, :, pl.ds(SPANS[h][0], SPANS[h][1] - SPANS[h][0])]
            second[k, h].append(send(src, R2[h].at[k, d - 1], on(b, d)))

    def f_act(k):
        halves = []
        for h in range(2):
            for copy in second[k, h]:
                copy.wait_recv()
            total = PB[k, x, y, :, columns(h)].astype(F32)
            for part in range(3):
                total = total + R2[h][k, part].astype(F32)
            halves.append(total)
        total = jnp.concatenate(halves, axis=1)
        squares = total[:, 3 * HID : 3 * HID + 1] + total[:, 3 * HID + 1 : 3 * HID + 2]
        inv = lax.rsqrt(squares / FULL_WIDTH + EPSILON)
        gate = total[:, :HID] * inv
        up = total[:, HID : 2 * HID] * inv
        back = total[:, BACK : BACK + HID]
        sig = jax.nn.sigmoid(gate)
        hidden = gate * sig * up
        dgate = back * up * sig * (1.0 + gate * (1.0 - sig))
        dup = back * gate * sig
        high = inv.astype(BF16).astype(F32)
        lane = lax.broadcasted_iota(jnp.int32, (16, 64), 1)
        tail = jnp.where(lane == 0, high, jnp.where(lane == 1, inv - high, 0.0))
        H[k, x, y] = jnp.concatenate([dgate, dup, hidden, tail], axis=1).astype(BF16)
        for h in range(2):
            gather2[k, h] = []
        for d in (2, 1, 3):
            for h in range(2):
                b = axes(k, h)[1]
                mine = H.at[k, x, y, :, pl.ds(SPANS[h][0], SPANS[h][1] - SPANS[h][0])]
                gather2[k, h].append(send(mine, mine, on(b, d)))

    def f_gather(k, h):
        a, b, ia, ib = axes(k, h)
        for copy in gather2[k, h]:
            copy.wait_recv()
        low, top = piece(H, k, h, ia, 0), piece(H, k, h, ia, 1)
        gather1[k, h] = (send(low, low, on(a, 1)), send(top, top, on(a, -1)))
        forward[k, h] = [send(top, top, on(a, 1)), send(low, low, on(a, -1))]

    def f_forward(k, h, side):
        a, b, ia, ib = axes(k, h)
        gather1[k, h][side].wait_recv()
        block = piece(H, k, h, lax.rem(ia + (3, 1)[side], 4), side)
        forward[k, h].append(send(block, block, on(a, (1, -1)[side])))

    def f_project(k):
        for h in range(2):
            for copy in forward[k, h]:
                copy.wait_recv()
        full = H[k].reshape(256, COLS)
        mlp = dot(full[:, BACK:], WD[...], ((1,), (0,))).astype(BF16)
        grad = dot(full[:, :BACK], WJ[...], ((1,), (0,))).astype(BF16)
        for who in (1, 0):
            for p in range(4):
                at_row = 64 * p + 32 * who
                Q[k, who, p, :, :WID] = mlp[at_row : at_row + 32]
                Q[k, who, p, :, WID:] = grad[at_row : at_row + 32]
        swap[k] = send(Q.at[k, 1], E.at[k], at(dc=1))

    landings = []

    def hand_on(d, to, sign):
        n = len(landings)
        landings.append(d)
        k, p = SLOT[d]
        return n, send(S.at[k, p], LAND.at[n], at(dz=d - to))

    def f_pair(k):
        swap[k].wait_recv()
        S[k] = (Q[k, 0].astype(F32) + E[k].astype(F32)).astype(BF16)
        for d in CHUNKS[k]:
            sign = 1 if d > 0 else -1
            if abs(d) == 2:
                last.append(hand_on(d, 0, sign))
            elif d and d % 2 == 0:
                even[d] = hand_on(d, d - sign, sign)

    def f_odd(d):
        k, p = SLOT[d]
        sign = 1 if d > 0 else -1
        total = S[k, p].astype(F32)
        for table, other in ((even, d + sign), (odd, d + 2 * sign)):
            if other in table:
                n, copy = table[other]
                copy.wait_recv()
                total = total + LAND[n].astype(F32)
        S[k, p] = total.astype(BF16)
        if abs(d) == 1 or abs(d) in DIRECT:
            last.append(hand_on(d, 0, sign))
        else:
            odd[d] = hand_on(d, d - 2 * sign, sign)

    started = []

    def f_grads(k):
        full = H[k].reshape(256, COLS)
        both = X[k].reshape(256, 2 * WID)
        inv = full[:, 3 * HID : 3 * HID + 1].astype(F32) + full[:, 3 * HID + 1 : 3 * HID + 2].astype(F32)
        normed = (both[:, :WID].astype(F32) * inv * gain()).astype(BF16)
        joined = dot(full[:, :BACK], normed, ((0,), (0,)))
        down = dot(full[:, BACK:], both[:, WID:], ((0,), (0,)))[:HID]
        if started:
            joined_ref[...] += joined
            down_ref[...] += down
        else:
            joined_ref[...] = joined
            down_ref[...] = down
        started.append(k)

    steps = {
        "X": f_pass, "A": f_partial, "B": f_merge, "C": f_second, "D": f_act, "E": f_gather, "F": f_forward,
        "G": f_project, "I": f_pair, "J": f_odd, "R": f_grads,
    }
    f_pass(0)
    for copy in fetch[3:]:
        copy.wait()
    for line in SCHEDULE:
        for step in line.split():
            numbers = (int(step[1:]),) if step[0] in "XJ" else tuple(int(c) for c in step[1:])
            steps[step[0]](*numbers)

    k, p = SLOT[0]
    total = S[k, p].astype(F32)
    for n, copy in last:
        copy.wait_recv()
        total = total + LAND[n].astype(F32)
    acts_ref[...] = total.astype(BF16)
    for copy in pending:
        copy.wait_send()


def deliver(acts, joined, down, out_ref, ig_ref, gg_ref, gu_ref, gd_ref, sems):
    copies = [
        pltpu.make_async_copy(src, dst, sems.at[i])
        for i, (src, dst) in enumerate((
            (joined.at[pl.ds(0, HID)], gg_ref),
            (joined.at[pl.ds(HID, HID)], gu_ref),
            (down, gd_ref),
            (acts.at[:, pl.ds(0, WID)], out_ref),
            (acts.at[:, pl.ds(WID, WID)], ig_ref),
        ))
    ]
    for copy in copies:
        copy.start()
    for copy in copies:
        copy.wait()


COPIES = 15 + 16 + 36 * 4 + 4 + 15


def shards(mantissa, block_exponents, norm_gain, gate_weight, up_weight, down_weight, cotangent):
    vmem = pl.BlockSpec(memory_space=pltpu.VMEM)
    hbm = pl.BlockSpec(memory_space=pltpu.HBM)
    widths = [b - a for a, b in SPANS]
    here = (mantissa, block_exponents, norm_gain, gate_weight.T, up_weight.T, down_weight, cotangent)
    here = [pltpu.with_memory_space_constraint(array, pltpu.HBM) for array in here]
    acts, joined, down = pl.pallas_call(
        layer,
        out_shape=(
            jax.ShapeDtypeStruct((32, 2 * WID), BF16),
            jax.ShapeDtypeStruct((BACK, WID), F32),
            jax.ShapeDtypeStruct((HID, WID), F32),
        ),
        in_specs=[hbm] * 7,
        out_specs=[vmem] * 3,
        scratch_shapes=[
            pltpu.VMEM((32, WID), BF16),
            pltpu.VMEM((32, WID), jnp.int32),
            pltpu.VMEM((WID,), BF16),
            pltpu.VMEM((4, 4, 2, 32, 2 * WID), BF16),
            pltpu.VMEM((BACK, WID), BF16),
            pltpu.VMEM((512, WID), BF16),
            pltpu.VMEM((4, 4, 4, 16, COLS), BF16),
            pltpu.VMEM((4, 6, 2, 16, widths[0]), BF16),
            pltpu.VMEM((4, 6, 2, 16, widths[1]), BF16),
            pltpu.VMEM((4, 3, 16, widths[0]), BF16),
            pltpu.VMEM((4, 3, 16, widths[1]), BF16),
            pltpu.VMEM((4, 4, 4, 16, COLS), BF16),
            pltpu.VMEM((4, 2, 4, 32, 2 * WID), BF16),
            pltpu.VMEM((4, 4, 32, 2 * WID), BF16),
            pltpu.VMEM((4, 4, 32, 2 * WID), BF16),
            pltpu.VMEM((15, 32, 2 * WID), BF16),
            pltpu.SemaphoreType.DMA((COPIES,)),
            pltpu.SemaphoreType.DMA((COPIES,)),
            pltpu.SemaphoreType.DMA((7,)),
        ],
        compiler_params=pltpu.CompilerParams(collective_id=0, has_side_effects=True, vmem_limit_bytes=48 << 20),
        name="swiglu_layer",
    )(*here)
    out, grad, gg, gu, gd = pl.pallas_call(
        deliver,
        out_shape=(
            jax.ShapeDtypeStruct((32, WID), BF16),
            jax.ShapeDtypeStruct((32, WID), BF16),
            jax.ShapeDtypeStruct((HID, WID), F32),
            jax.ShapeDtypeStruct((HID, WID), F32),
            jax.ShapeDtypeStruct((HID, WID), F32),
        ),
        in_specs=[vmem] * 3,
        out_specs=[hbm] * 5,
        scratch_shapes=[pltpu.SemaphoreType.DMA((5,))],
        compiler_params=pltpu.CompilerParams(vmem_limit_bytes=2 << 20),
        name="deliver",
    )(acts, joined, down)
    return out, grad, gg.T, gu.T, gd


def solution(mesh):
    in_specs = (
        P("tensor", "dp"),
        P("tensor", None),
        P("dp"),
        P("dp", "tensor"),
        P("dp", "tensor"),
        P("tensor", "dp"),
        P("tensor", "dp"),
    )
    out_specs = (
        P("tensor", "dp"),
        P("tensor", "dp"),
        P("dp", "tensor"),
        P("dp", "tensor"),
        P("tensor", "dp"),
    )
    return jax.shard_map(shards, mesh=mesh, in_specs=in_specs, out_specs=out_specs, check_vma=False)
```

```python
import jax
import jax.numpy as jnp
from jax import lax
from jax.experimental import pallas as pl
from jax.experimental.pallas import tpu as pltpu
from jax.sharding import PartitionSpec as P

BLOCK = 16
EPSILON = 1e-05
FULL_WIDTH = 4096
MESH = pl.DeviceIdType.MESH
F32, BF16 = jnp.float32, jnp.bfloat16

NX, NY, NZ = 4, 4, 16
HID = 448
WID = 256
COLS = 1408
BACK = 2 * HID
SPANS = ((0, 768), (768, 1408))

CHUNKS = ((0, 1, -1, 2), (-2, 3, -3, 4), (-4, 5, -5, 6), (-6, 7, -7, 8))
SLOT = {d: (k, p) for k, ds in enumerate(CHUNKS) for p, d in enumerate(ds)}
DIRECT = (5,)
SCHEDULE = (
    "X-1 X1 X-2 X2",
    "A0 X-3 X3 X-4",
    "X4 B000 B001 B010",
    "B011 A1 X-5 X5",
    "X-6 X6 C00 C01",
    "A2 B110 B111 B100",
    "B101 X-7 X7 X8",
    "D0 A3 B210 B200",
    "B201 B211 C10 C11",
    "E00 E01 B300 B301",
    "B310 B311 C21 C20",
    "D1 F010 F011 F000",
    "F001 C30 C31 D2",
    "E11 E10 G0 D3",
    "I0 E21 E20 F100",
    "F101 F110 F111 E31",
    "E30 F210 F211 F200",
    "F201 G1 F300 F301",
    "F310 F311 I1 G2",
    "G3 I2 J3 I3",
    "J-7 J-3 J1 J7",
    "J-5 J-1 J5 R0",
    "R1 R2 R3",
)


def dot(a, b, dims):
    return lax.dot_general(a, b, (dims, ((), ())), preferred_element_type=F32)


def rounded(total):
    tail = total[:, -128:]
    lane = lax.broadcasted_iota(jnp.int32, tail.shape, 1)
    lost = pltpu.roll(tail - tail.astype(BF16).astype(F32), 1, 1)
    tail = tail + jnp.where(lane == 65, lost, 0.0)
    return jnp.concatenate([total[:, :-128], tail], axis=1).astype(BF16)


def layer(
    m_hbm, e_hbm, g_hbm, wg_hbm, wu_hbm, wd_hbm, c_hbm,
    acts_ref, joined_ref, down_ref,
    MV, EV, g_ref, X, WJ, WD, PB, R1A, R1B, R2A, R2B, H, Q, E, S, LAND, ss, rs, ls,
):
    dp, tn = lax.axis_index("dp"), lax.axis_index("tensor")
    x, y = dp // NY, lax.rem(dp, NY)
    z, core = tn // 2, lax.rem(tn, 2)
    R1, R2 = (R1A, R1B), (R2A, R2B)

    def at(dx=0, dy=0, dz=0, dc=0):
        px, py = lax.rem(x + dx + NX, NX), lax.rem(y + dy + NY, NY)
        pz, pc = lax.rem(z + dz + NZ, NZ), lax.rem(core + dc, 2)
        return (px * NY + py, pz * 2 + pc)

    def on(axis, d):
        return at(dx=d) if axis == "x" else at(dy=d)

    counter = [0]
    pending = []

    def send(src, dst, device):
        n = counter[0]
        counter[0] += 1
        copy = pltpu.make_async_remote_copy(
            src_ref=src, dst_ref=dst, send_sem=ss.at[n], recv_sem=rs.at[n], device_id=device, device_id_type=MESH
        )
        copy.start()
        pending.append(copy)
        return copy

    barrier = pltpu.get_barrier_semaphore()
    near = [at(dc=1)] + [at(dz=d) for d in (1, 2, -1, -2)]
    near += [at(dx=d) for d in (1, 2, 3)] + [at(dy=d) for d in (1, 2, 3)]
    for device in near:
        pl.semaphore_signal(barrier, inc=1, device_id=device, device_id_type=MESH)

    own = X.at[SLOT[0][0], SLOT[0][1], 0]
    fetch = [
        pltpu.make_async_copy(src, dst, ls.at[i])
        for i, (src, dst) in enumerate((
            (m_hbm, MV),
            (e_hbm, EV),
            (c_hbm, own.at[:, pl.ds(WID, WID)]),
            (wg_hbm, WJ.at[pl.ds(0, HID)]),
            (wu_hbm, WJ.at[pl.ds(HID, HID)]),
            (wd_hbm, WD.at[pl.ds(0, HID)]),
            (g_hbm, g_ref),
        ))
    ]
    for copy in fetch:
        copy.start()
    row = lax.broadcasted_iota(jnp.int32, (WID, WID), 0)
    col = lax.broadcasted_iota(jnp.int32, (WID, WID), 1)
    pick = jnp.where(row == dp * (WID // BLOCK) + col // BLOCK, 1.0, 0.0).astype(BF16)
    WD[HID:] = jnp.zeros((64, WID), BF16)

    for copy in fetch[:3]:
        copy.wait()
    exponents = EV[...]
    scales = jnp.zeros(exponents.shape, F32)
    for level in range(-2, 4):
        scales = scales + jnp.where(exponents == level, 2.0**level, 0.0)
    scales = dot(scales.astype(BF16), pick, ((1,), (0,)))
    own[:, :WID] = (MV[...].astype(F32) * scales).astype(BF16)

    pl.semaphore_wait(barrier, len(near))

    ring = {}
    twin = {}

    def xat(d, who):
        return X.at[SLOT[d][0], SLOT[d][1], who]

    def f_pass(d):
        if d != 0:
            ring[d].wait_recv()
        for step in (2, -1, 1, -2) if d == 0 else (-2,) if d < 0 else (2,):
            if -8 < d + step < 9:
                ring[d + step] = send(xat(d, 0), xat(d + step, 0), at(dz=-step))
        twin[d] = send(xat(d, 0), xat(d, 1), at(dc=1))

    def gain():
        return g_ref[...].astype(F32).reshape(1, WID)

    first, direct, second, gather2, gather1, forward = {}, {}, {}, {}, {}, {}
    swap, even, odd, last = {}, {}, {}, []

    def axes(k, h):
        return ("x", "y", x, y) if (k + h) % 2 == 0 else ("y", "x", y, x)

    def columns(h):
        return slice(*SPANS[h])

    def spot(k, h, index, half):
        two = pl.ds(2 * half, 2)
        return (k, index, two) if axes(k, h)[0] == "x" else (k, two, index)

    def piece(ref, k, h, index, half):
        a, b, c = spot(k, h, index, half)
        return ref.at[a, b, c, :, pl.ds(SPANS[h][0], SPANS[h][1] - SPANS[h][0])]

    def f_partial(k):
        for d in CHUNKS[k]:
            twin[d].wait_recv()
        both = X[k].reshape(256, 2 * WID)
        values = both[:, :WID].astype(F32)
        scaled = (values * gain()).astype(BF16)
        joined = dot(scaled, WJ[...], ((1,), (1,)))
        PB[k, :, :, :, :BACK] = joined.astype(BF16).reshape(4, 4, 16, BACK)
        def send_far(h):
            a, b, ia, ib = axes(k, h)
            far = lax.rem(ia + 2, 4)
            first[k, h] = (
                send(piece(PB, k, h, far, 0), R1[h].at[k, 0], on(a, 1)),
                send(piece(PB, k, h, far, 1), R1[h].at[k, 1], on(a, -1)),
            )

        send_far(0)
        back = dot(both[:, WID:], WD[...], ((1,), (1,)))
        lane = lax.broadcasted_iota(jnp.int32, back.shape, 1)
        squares = jnp.sum(values * values, axis=1, keepdims=True)
        high = squares.astype(BF16).astype(F32)
        back = jnp.where(lane == HID, high, jnp.where(lane == HID + 1, squares - high, back))
        PB[k, :, :, :, BACK:] = back.astype(BF16).reshape(4, 4, 16, 512)
        send_far(1)
        for h in range(2):
            a, b, ia, ib = axes(k, h)
            right, left = lax.rem(ia + 1, 4), lax.rem(ia + 3, 4)
            direct[k, h] = [
                send(piece(PB, k, h, right, 1), R1[h].at[k, 2], on(a, 1)),
                send(piece(PB, k, h, left, 0), R1[h].at[k, 3], on(a, -1)),
            ]

    def add_up(k, h, index, half, parts):
        a, b, c = spot(k, h, index, half)
        width = SPANS[h][1] - SPANS[h][0]
        total = PB[a, b, c, :, columns(h)].astype(F32)
        for part in parts:
            total = total + R1[h][k, part].astype(F32)
        total = total.reshape(32, width)
        total = rounded(total) if h == 1 else total.astype(BF16)
        PB[a, b, c, :, columns(h)] = total.reshape(2, 16, width)

    def f_merge(k, h, side):
        a, b, ia, ib = axes(k, h)
        to = lax.rem(ia + (1, 3)[side], 4)
        first[k, h][side].wait_recv()
        add_up(k, h, to, side, (side,))
        direct[k, h].append(send(piece(PB, k, h, to, side), R1[h].at[k, 4 + side], on(a, (1, -1)[side])))

    def f_second(k, h):
        a, b, ia, ib = axes(k, h)
        for copy in direct[k, h]:
            copy.wait_recv()
        add_up(k, h, ia, 0, (4, 3))
        add_up(k, h, ia, 1, (2, 5))
        second[k, h] = []
        for d in (2, 1, 3):
            to = lax.rem(ib + d, 4)
            px, py = (ia, to) if a == "x" else (to, ia)
            src = PB.at[k, px, py, :, pl.ds(SPANS[h][0], SPANS[h][1] - SPANS[h][0])]
            second[k, h].append(send(src, R2[h].at[k, d - 1], on(b, d)))

    def f_act(k):
        halves = []
        for h in range(2):
            for copy in second[k, h]:
                copy.wait_recv()
            total = PB[k, x, y, :, columns(h)].astype(F32)
            for part in range(3):
                total = total + R2[h][k, part].astype(F32)
            halves.append(total)
        total = jnp.concatenate(halves, axis=1)
        squares = total[:, 3 * HID : 3 * HID + 1] + total[:, 3 * HID + 1 : 3 * HID + 2]
        inv = lax.rsqrt(squares / FULL_WIDTH + EPSILON)
        gate = total[:, :HID] * inv
        up = total[:, HID : 2 * HID] * inv
        back = total[:, BACK : BACK + HID]
        sig = jax.nn.sigmoid(gate)
        hidden = gate * sig * up
        dgate = back * up * sig * (1.0 + gate * (1.0 - sig))
        dup = back * gate * sig
        high = inv.astype(BF16).astype(F32)
        lane = lax.broadcasted_iota(jnp.int32, (16, 64), 1)
        tail = jnp.where(lane == 0, high, jnp.where(lane == 1, inv - high, 0.0))
        H[k, x, y] = jnp.concatenate([dgate, dup, hidden, tail], axis=1).astype(BF16)
        for h in range(2):
            gather2[k, h] = []
        for d in (2, 1, 3):
            for h in range(2):
                b = axes(k, h)[1]
                mine = H.at[k, x, y, :, pl.ds(SPANS[h][0], SPANS[h][1] - SPANS[h][0])]
                gather2[k, h].append(send(mine, mine, on(b, d)))

    def f_gather(k, h):
        a, b, ia, ib = axes(k, h)
        for copy in gather2[k, h]:
            copy.wait_recv()
        low, top = piece(H, k, h, ia, 0), piece(H, k, h, ia, 1)
        gather1[k, h] = (send(low, low, on(a, 1)), send(top, top, on(a, -1)))
        forward[k, h] = [send(top, top, on(a, 1)), send(low, low, on(a, -1))]

    def f_forward(k, h, side):
        a, b, ia, ib = axes(k, h)
        gather1[k, h][side].wait_recv()
        block = piece(H, k, h, lax.rem(ia + (3, 1)[side], 4), side)
        forward[k, h].append(send(block, block, on(a, (1, -1)[side])))

    def f_project(k):
        for h in range(2):
            for copy in forward[k, h]:
                copy.wait_recv()
        full = H[k].reshape(256, COLS)
        mlp = dot(full[:, BACK:], WD[...], ((1,), (0,))).astype(BF16)
        grad = dot(full[:, :BACK], WJ[...], ((1,), (0,))).astype(BF16)
        for who in (1, 0):
            for p in range(4):
                at_row = 64 * p + 32 * who
                Q[k, who, p, :, :WID] = mlp[at_row : at_row + 32]
                Q[k, who, p, :, WID:] = grad[at_row : at_row + 32]
        swap[k] = send(Q.at[k, 1], E.at[k], at(dc=1))

    landings = []

    def hand_on(d, to, sign):
        n = len(landings)
        landings.append(d)
        k, p = SLOT[d]
        return n, send(S.at[k, p], LAND.at[n], at(dz=d - to))

    def f_pair(k):
        swap[k].wait_recv()
        S[k] = (Q[k, 0].astype(F32) + E[k].astype(F32)).astype(BF16)
        for d in CHUNKS[k]:
            sign = 1 if d > 0 else -1
            if abs(d) == 2:
                last.append(hand_on(d, 0, sign))
            elif d and d % 2 == 0:
                even[d] = hand_on(d, d - sign, sign)

    def f_odd(d):
        k, p = SLOT[d]
        sign = 1 if d > 0 else -1
        total = S[k, p].astype(F32)
        for table, other in ((even, d + sign), (odd, d + 2 * sign)):
            if other in table:
                n, copy = table[other]
                copy.wait_recv()
                total = total + LAND[n].astype(F32)
        S[k, p] = total.astype(BF16)
        if abs(d) == 1 or abs(d) in DIRECT:
            last.append(hand_on(d, 0, sign))
        else:
            odd[d] = hand_on(d, d - 2 * sign, sign)

    started = []

    def f_grads(k):
        full = H[k].reshape(256, COLS)
        both = X[k].reshape(256, 2 * WID)
        inv = full[:, 3 * HID : 3 * HID + 1].astype(F32) + full[:, 3 * HID + 1 : 3 * HID + 2].astype(F32)
        normed = (both[:, :WID].astype(F32) * inv * gain()).astype(BF16)
        joined = dot(full[:, :BACK], normed, ((0,), (0,)))
        down = dot(full[:, BACK:], both[:, WID:], ((0,), (0,)))[:HID]
        if started:
            joined_ref[...] += joined
            down_ref[...] += down
        else:
            joined_ref[...] = joined
            down_ref[...] = down
        started.append(k)

    steps = {
        "X": f_pass, "A": f_partial, "B": f_merge, "C": f_second, "D": f_act, "E": f_gather, "F": f_forward,
        "G": f_project, "I": f_pair, "J": f_odd, "R": f_grads,
    }
    f_pass(0)
    for copy in fetch[3:]:
        copy.wait()
    for line in SCHEDULE:
        for step in line.split():
            numbers = (int(step[1:]),) if step[0] in "XJ" else tuple(int(c) for c in step[1:])
            steps[step[0]](*numbers)

    k, p = SLOT[0]
    total = S[k, p].astype(F32)
    for n, copy in last:
        copy.wait_recv()
        total = total + LAND[n].astype(F32)
    acts_ref[...] = total.astype(BF16)
    for copy in pending:
        copy.wait_send()


def deliver(acts, joined, down, out_ref, ig_ref, gg_ref, gu_ref, gd_ref, sems):
    copies = [
        pltpu.make_async_copy(src, dst, sems.at[i])
        for i, (src, dst) in enumerate((
            (joined.at[pl.ds(0, HID)], gg_ref),
            (joined.at[pl.ds(HID, HID)], gu_ref),
            (down, gd_ref),
            (acts.at[:, pl.ds(0, WID)], out_ref),
            (acts.at[:, pl.ds(WID, WID)], ig_ref),
        ))
    ]
    for copy in copies:
        copy.start()
    for copy in copies:
        copy.wait()


COPIES = 15 + 16 + 36 * 4 + 4 + 15


def shards(mantissa, block_exponents, norm_gain, gate_weight, up_weight, down_weight, cotangent):
    vmem = pl.BlockSpec(memory_space=pltpu.VMEM)
    hbm = pl.BlockSpec(memory_space=pltpu.HBM)
    widths = [b - a for a, b in SPANS]
    here = (mantissa, block_exponents, norm_gain, gate_weight.T, up_weight.T, down_weight, cotangent)
    here = [pltpu.with_memory_space_constraint(array, pltpu.HBM) for array in here]
    acts, joined, down = pl.pallas_call(
        layer,
        out_shape=(
            jax.ShapeDtypeStruct((32, 2 * WID), BF16),
            jax.ShapeDtypeStruct((BACK, WID), F32),
            jax.ShapeDtypeStruct((HID, WID), F32),
        ),
        in_specs=[hbm] * 7,
        out_specs=[vmem] * 3,
        scratch_shapes=[
            pltpu.VMEM((32, WID), BF16),
            pltpu.VMEM((32, WID), jnp.int32),
            pltpu.VMEM((WID,), BF16),
            pltpu.VMEM((4, 4, 2, 32, 2 * WID), BF16),
            pltpu.VMEM((BACK, WID), BF16),
            pltpu.VMEM((512, WID), BF16),
            pltpu.VMEM((4, 4, 4, 16, COLS), BF16),
            pltpu.VMEM((4, 6, 2, 16, widths[0]), BF16),
            pltpu.VMEM((4, 6, 2, 16, widths[1]), BF16),
            pltpu.VMEM((4, 3, 16, widths[0]), BF16),
            pltpu.VMEM((4, 3, 16, widths[1]), BF16),
            pltpu.VMEM((4, 4, 4, 16, COLS), BF16),
            pltpu.VMEM((4, 2, 4, 32, 2 * WID), BF16),
            pltpu.VMEM((4, 4, 32, 2 * WID), BF16),
            pltpu.VMEM((4, 4, 32, 2 * WID), BF16),
            pltpu.VMEM((15, 32, 2 * WID), BF16),
            pltpu.SemaphoreType.DMA((COPIES,)),
            pltpu.SemaphoreType.DMA((COPIES,)),
            pltpu.SemaphoreType.DMA((7,)),
        ],
        compiler_params=pltpu.CompilerParams(collective_id=0, has_side_effects=True, vmem_limit_bytes=48 << 20),
        name="swiglu_layer",
    )(*here)
    out, grad, gg, gu, gd = pl.pallas_call(
        deliver,
        out_shape=(
            jax.ShapeDtypeStruct((32, WID), BF16),
            jax.ShapeDtypeStruct((32, WID), BF16),
            jax.ShapeDtypeStruct((HID, WID), F32),
            jax.ShapeDtypeStruct((HID, WID), F32),
            jax.ShapeDtypeStruct((HID, WID), F32),
        ),
        in_specs=[vmem] * 3,
        out_specs=[hbm] * 5,
        scratch_shapes=[pltpu.SemaphoreType.DMA((5,))],
        compiler_params=pltpu.CompilerParams(vmem_limit_bytes=2 << 20),
        name="deliver",
    )(acts, joined, down)
    return out, grad, gg.T, gu.T, gd


def solution(mesh):
    in_specs = (
        P("tensor", "dp"),
        P("tensor", None),
        P("dp"),
        P("dp", "tensor"),
        P("dp", "tensor"),
        P("tensor", "dp"),
        P("tensor", "dp"),
    )
    out_specs = (
        P("tensor", "dp"),
        P("tensor", "dp"),
        P("dp", "tensor"),
        P("dp", "tensor"),
        P("tensor", "dp"),
    )
    return jax.shard_map(shards, mesh=mesh, in_specs=in_specs, out_specs=out_specs, check_vma=False)
```

```python
import jax
import jax.numpy as jnp
from jax import lax
from jax.experimental import pallas as pl
from jax.experimental.pallas import tpu as pltpu
from jax.sharding import PartitionSpec as P

BLOCK = 16
EPSILON = 1e-05
FULL_WIDTH = 4096
MESH = pl.DeviceIdType.MESH
F32, BF16 = jnp.float32, jnp.bfloat16

NX, NY, NZ = 4, 4, 16
HID = 448
WID = 256
COLS = 1408
BACK = 2 * HID
SPANS = ((0, 640), (640, 1408))

CHUNKS = ((0, 1, -1, 2), (-2, 3, -3, 4), (-4, 5, -5, 6), (-6, 7, -7, 8))
SLOT = {d: (k, p) for k, ds in enumerate(CHUNKS) for p, d in enumerate(ds)}
DIRECT = (5,)
SCHEDULE = (
    "X-1 X1 X-2 X2",
    "A0 X-3 X3 X-4",
    "X4 B000 B001 A1",
    "B010 X5 X-5 B011",
    "X-6 X6 C00 B100",
    "B101 A2 X7 B110",
    "X-7 B111 C01 X8",
    "A3 C10 B200 B201",
    "B210 B211 C11 D0",
    "B300 B301 B310 B311",
    "C21 D1 C20 E00",
    "C30 E01 C31 E11",
    "D2 E10 F010 F011",
    "F000 F001 D3 F110",
    "F111 E20 F100 F101",
    "E21 G0 R0 E30",
    "E31 G1 I0 R1",
    "F200 F201 F210 F211",
    "I1 F310 F311 F300",
    "F301 G2 J3 R2",
    "G3 R3 I2 I3",
    "J-7 J1 J-3 J7",
    "J-5 J-1 J5",
)


def dot(a, b, dims):
    return lax.dot_general(a, b, (dims, ((), ())), preferred_element_type=F32)


def rounded(total):
    tail = total[:, -128:]
    lane = lax.broadcasted_iota(jnp.int32, tail.shape, 1)
    lost = pltpu.roll(tail - tail.astype(BF16).astype(F32), 1, 1)
    tail = tail + jnp.where(lane == 65, lost, 0.0)
    return jnp.concatenate([total[:, :-128], tail], axis=1).astype(BF16)


def layer(
    m_hbm, e_hbm, g_hbm, wg_hbm, wu_hbm, wd_hbm, c_hbm,
    acts_ref, joined_ref, down_ref,
    MV, EV, g_ref, X, WJ, WD, PB, R1A, R1B, R2A, R2B, H, Q, E, S, LAND, ss, rs, ls,
):
    dp, tn = lax.axis_index("dp"), lax.axis_index("tensor")
    x, y = dp // NY, lax.rem(dp, NY)
    z, core = tn // 2, lax.rem(tn, 2)
    R1, R2 = (R1A, R1B), (R2A, R2B)

    def at(dx=0, dy=0, dz=0, dc=0):
        px, py = lax.rem(x + dx + NX, NX), lax.rem(y + dy + NY, NY)
        pz, pc = lax.rem(z + dz + NZ, NZ), lax.rem(core + dc, 2)
        return (px * NY + py, pz * 2 + pc)

    def on(axis, d):
        return at(dx=d) if axis == "x" else at(dy=d)

    counter = [0]
    pending = []

    def send(src, dst, device):
        n = counter[0]
        counter[0] += 1
        copy = pltpu.make_async_remote_copy(
            src_ref=src, dst_ref=dst, send_sem=ss.at[n], recv_sem=rs.at[n], device_id=device, device_id_type=MESH
        )
        copy.start()
        pending.append(copy)
        return copy

    barrier = pltpu.get_barrier_semaphore()
    near = [at(dc=1)] + [at(dz=d) for d in (1, 2, -1, -2)]
    near += [at(dx=d) for d in (1, 2, 3)] + [at(dy=d) for d in (1, 2, 3)]
    for device in near:
        pl.semaphore_signal(barrier, inc=1, device_id=device, device_id_type=MESH)

    own = X.at[SLOT[0][0], SLOT[0][1], 0]
    fetch = [
        pltpu.make_async_copy(src, dst, ls.at[i])
        for i, (src, dst) in enumerate((
            (m_hbm, MV),
            (e_hbm, EV),
            (c_hbm, own.at[:, pl.ds(WID, WID)]),
            (wg_hbm, WJ.at[pl.ds(0, HID)]),
            (wu_hbm, WJ.at[pl.ds(HID, HID)]),
            (wd_hbm, WD.at[pl.ds(0, HID)]),
            (g_hbm, g_ref),
        ))
    ]
    for copy in fetch:
        copy.start()
    row = lax.broadcasted_iota(jnp.int32, (WID, WID), 0)
    col = lax.broadcasted_iota(jnp.int32, (WID, WID), 1)
    pick = jnp.where(row == dp * (WID // BLOCK) + col // BLOCK, 1.0, 0.0).astype(BF16)
    WD[HID:] = jnp.zeros((64, WID), BF16)

    for copy in fetch[:3]:
        copy.wait()
    exponents = EV[...]
    scales = jnp.zeros(exponents.shape, F32)
    for level in range(-2, 4):
        scales = scales + jnp.where(exponents == level, 2.0**level, 0.0)
    scales = dot(scales.astype(BF16), pick, ((1,), (0,)))
    own[:, :WID] = (MV[...].astype(F32) * scales).astype(BF16)

    pl.semaphore_wait(barrier, len(near))

    ring = {}
    twin = {}

    def xat(d, who):
        return X.at[SLOT[d][0], SLOT[d][1], who]

    def f_pass(d):
        if d != 0:
            ring[d].wait_recv()
        for step in (-1, 1, -2, 2) if d == 0 else (-2,) if d < 0 else (2,):
            if -8 < d + step < 9:
                ring[d + step] = send(xat(d, 0), xat(d + step, 0), at(dz=-step))
        twin[d] = send(xat(d, 0), xat(d, 1), at(dc=1))

    def gain():
        return g_ref[...].astype(F32).reshape(1, WID)

    first, direct, second, gather2, gather1, forward = {}, {}, {}, {}, {}, {}
    swap, even, odd, last = {}, {}, {}, []

    def axes(k, h):
        return ("x", "y", x, y) if (k + h) % 2 == 0 else ("y", "x", y, x)

    def columns(h):
        return slice(*SPANS[h])

    def spot(k, h, index, half):
        two = pl.ds(2 * half, 2)
        return (k, index, two) if axes(k, h)[0] == "x" else (k, two, index)

    def piece(ref, k, h, index, half):
        a, b, c = spot(k, h, index, half)
        return ref.at[a, b, c, :, pl.ds(SPANS[h][0], SPANS[h][1] - SPANS[h][0])]

    def f_partial(k):
        for d in CHUNKS[k]:
            twin[d].wait_recv()
        both = X[k].reshape(256, 2 * WID)
        values = both[:, :WID].astype(F32)
        scaled = (values * gain()).astype(BF16)
        joined = dot(scaled, WJ[...], ((1,), (1,)))
        PB[k, :, :, :, :BACK] = joined.astype(BF16).reshape(4, 4, 16, BACK)
        def send_far(h):
            a, b, ia, ib = axes(k, h)
            far = lax.rem(ia + 2, 4)
            first[k, h] = (
                send(piece(PB, k, h, far, 0), R1[h].at[k, 0], on(a, 1)),
                send(piece(PB, k, h, far, 1), R1[h].at[k, 1], on(a, -1)),
            )

        send_far(0)
        back = dot(both[:, WID:], WD[...], ((1,), (1,)))
        lane = lax.broadcasted_iota(jnp.int32, back.shape, 1)
        squares = jnp.sum(values * values, axis=1, keepdims=True)
        high = squares.astype(BF16).astype(F32)
        back = jnp.where(lane == HID, high, jnp.where(lane == HID + 1, squares - high, back))
        PB[k, :, :, :, BACK:] = back.astype(BF16).reshape(4, 4, 16, 512)
        send_far(1)
        for h in range(2):
            a, b, ia, ib = axes(k, h)
            right, left = lax.rem(ia + 1, 4), lax.rem(ia + 3, 4)
            direct[k, h] = [
                send(piece(PB, k, h, right, 1), R1[h].at[k, 2], on(a, 1)),
                send(piece(PB, k, h, left, 0), R1[h].at[k, 3], on(a, -1)),
            ]

    def add_up(k, h, index, half, parts):
        a, b, c = spot(k, h, index, half)
        width = SPANS[h][1] - SPANS[h][0]
        total = PB[a, b, c, :, columns(h)].astype(F32)
        for part in parts:
            total = total + R1[h][k, part].astype(F32)
        total = total.reshape(32, width)
        total = rounded(total) if h == 1 else total.astype(BF16)
        PB[a, b, c, :, columns(h)] = total.reshape(2, 16, width)

    def f_merge(k, h, side):
        a, b, ia, ib = axes(k, h)
        to = lax.rem(ia + (1, 3)[side], 4)
        first[k, h][side].wait_recv()
        add_up(k, h, to, side, (side,))
        direct[k, h].append(send(piece(PB, k, h, to, side), R1[h].at[k, 4 + side], on(a, (1, -1)[side])))

    def f_second(k, h):
        a, b, ia, ib = axes(k, h)
        for copy in direct[k, h]:
            copy.wait_recv()
        add_up(k, h, ia, 0, (4, 3))
        add_up(k, h, ia, 1, (2, 5))
        second[k, h] = []
        for d in (2, 1, 3):
            to = lax.rem(ib + d, 4)
            px, py = (ia, to) if a == "x" else (to, ia)
            src = PB.at[k, px, py, :, pl.ds(SPANS[h][0], SPANS[h][1] - SPANS[h][0])]
            second[k, h].append(send(src, R2[h].at[k, d - 1], on(b, d)))

    def f_act(k):
        halves = []
        for h in range(2):
            for copy in second[k, h]:
                copy.wait_recv()
            total = PB[k, x, y, :, columns(h)].astype(F32)
            for part in range(3):
                total = total + R2[h][k, part].astype(F32)
            halves.append(total)
        total = jnp.concatenate(halves, axis=1)
        squares = total[:, 3 * HID : 3 * HID + 1] + total[:, 3 * HID + 1 : 3 * HID + 2]
        inv = lax.rsqrt(squares / FULL_WIDTH + EPSILON)
        gate = total[:, :HID] * inv
        up = total[:, HID : 2 * HID] * inv
        back = total[:, BACK : BACK + HID]
        sig = jax.nn.sigmoid(gate)
        hidden = gate * sig * up
        dgate = back * up * sig * (1.0 + gate * (1.0 - sig))
        dup = back * gate * sig
        high = inv.astype(BF16).astype(F32)
        lane = lax.broadcasted_iota(jnp.int32, (16, 64), 1)
        tail = jnp.where(lane == 0, high, jnp.where(lane == 1, inv - high, 0.0))
        H[k, x, y] = jnp.concatenate([dgate, dup, hidden, tail], axis=1).astype(BF16)
        for h in range(2):
            gather2[k, h] = []
        for d in (2, 1, 3):
            for h in range(2):
                b = axes(k, h)[1]
                mine = H.at[k, x, y, :, pl.ds(SPANS[h][0], SPANS[h][1] - SPANS[h][0])]
                gather2[k, h].append(send(mine, mine, on(b, d)))

    def f_gather(k, h):
        a, b, ia, ib = axes(k, h)
        for copy in gather2[k, h]:
            copy.wait_recv()
        low, top = piece(H, k, h, ia, 0), piece(H, k, h, ia, 1)
        gather1[k, h] = (send(low, low, on(a, 1)), send(top, top, on(a, -1)))
        forward[k, h] = [send(top, top, on(a, 1)), send(low, low, on(a, -1))]

    def f_forward(k, h, side):
        a, b, ia, ib = axes(k, h)
        gather1[k, h][side].wait_recv()
        block = piece(H, k, h, lax.rem(ia + (3, 1)[side], 4), side)
        forward[k, h].append(send(block, block, on(a, (1, -1)[side])))

    def f_project(k):
        for h in range(2):
            for copy in forward[k, h]:
                copy.wait_recv()
        full = H[k].reshape(256, COLS)
        mlp = dot(full[:, BACK:], WD[...], ((1,), (0,))).astype(BF16)
        grad = dot(full[:, :BACK], WJ[...], ((1,), (0,))).astype(BF16)
        for who in (1, 0):
            for p in range(4):
                at_row = 64 * p + 32 * who
                Q[k, who, p, :, :WID] = mlp[at_row : at_row + 32]
                Q[k, who, p, :, WID:] = grad[at_row : at_row + 32]
        swap[k] = send(Q.at[k, 1], E.at[k], at(dc=1))

    landings = []

    def hand_on(d, to, sign):
        n = len(landings)
        landings.append(d)
        k, p = SLOT[d]
        return n, send(S.at[k, p], LAND.at[n], at(dz=d - to))

    def f_pair(k):
        swap[k].wait_recv()
        S[k] = (Q[k, 0].astype(F32) + E[k].astype(F32)).astype(BF16)
        for d in CHUNKS[k]:
            sign = 1 if d > 0 else -1
            if abs(d) == 2:
                last.append(hand_on(d, 0, sign))
            elif d and d % 2 == 0:
                even[d] = hand_on(d, d - sign, sign)

    def f_odd(d):
        k, p = SLOT[d]
        sign = 1 if d > 0 else -1
        total = S[k, p].astype(F32)
        for table, other in ((even, d + sign), (odd, d + 2 * sign)):
            if other in table:
                n, copy = table[other]
                copy.wait_recv()
                total = total + LAND[n].astype(F32)
        S[k, p] = total.astype(BF16)
        if abs(d) == 1 or abs(d) in DIRECT:
            last.append(hand_on(d, 0, sign))
        else:
            odd[d] = hand_on(d, d - 2 * sign, sign)

    started = []

    def f_grads(k):
        full = H[k].reshape(256, COLS)
        both = X[k].reshape(256, 2 * WID)
        inv = full[:, 3 * HID : 3 * HID + 1].astype(F32) + full[:, 3 * HID + 1 : 3 * HID + 2].astype(F32)
        normed = (both[:, :WID].astype(F32) * inv * gain()).astype(BF16)
        joined = dot(full[:, :BACK], normed, ((0,), (0,)))
        down = dot(full[:, BACK:], both[:, WID:], ((0,), (0,)))[:HID]
        if started:
            joined_ref[...] += joined
            down_ref[...] += down
        else:
            joined_ref[...] = joined
            down_ref[...] = down
        started.append(k)

    steps = {
        "X": f_pass, "A": f_partial, "B": f_merge, "C": f_second, "D": f_act, "E": f_gather, "F": f_forward,
        "G": f_project, "I": f_pair, "J": f_odd, "R": f_grads,
    }
    f_pass(0)
    for copy in fetch[3:]:
        copy.wait()
    for line in SCHEDULE:
        for step in line.split():
            numbers = (int(step[1:]),) if step[0] in "XJ" else tuple(int(c) for c in step[1:])
            steps[step[0]](*numbers)

    k, p = SLOT[0]
    total = S[k, p].astype(F32)
    for n, copy in last:
        copy.wait_recv()
        total = total + LAND[n].astype(F32)
    acts_ref[...] = total.astype(BF16)
    for copy in pending:
        copy.wait_send()


def deliver(acts, joined, down, out_ref, ig_ref, gg_ref, gu_ref, gd_ref, sems):
    copies = [
        pltpu.make_async_copy(src, dst, sems.at[i])
        for i, (src, dst) in enumerate((
            (joined.at[pl.ds(0, HID)], gg_ref),
            (joined.at[pl.ds(HID, HID)], gu_ref),
            (down, gd_ref),
            (acts.at[:, pl.ds(0, WID)], out_ref),
            (acts.at[:, pl.ds(WID, WID)], ig_ref),
        ))
    ]
    for copy in copies:
        copy.start()
    for copy in copies:
        copy.wait()


COPIES = 15 + 16 + 36 * 4 + 4 + 15


def shards(mantissa, block_exponents, norm_gain, gate_weight, up_weight, down_weight, cotangent):
    vmem = pl.BlockSpec(memory_space=pltpu.VMEM)
    hbm = pl.BlockSpec(memory_space=pltpu.HBM)
    widths = [b - a for a, b in SPANS]
    here = (mantissa, block_exponents, norm_gain, gate_weight.T, up_weight.T, down_weight, cotangent)
    here = [pltpu.with_memory_space_constraint(array, pltpu.HBM) for array in here]
    acts, joined, down = pl.pallas_call(
        layer,
        out_shape=(
            jax.ShapeDtypeStruct((32, 2 * WID), BF16),
            jax.ShapeDtypeStruct((BACK, WID), F32),
            jax.ShapeDtypeStruct((HID, WID), F32),
        ),
        in_specs=[hbm] * 7,
        out_specs=[vmem] * 3,
        scratch_shapes=[
            pltpu.VMEM((32, WID), BF16),
            pltpu.VMEM((32, WID), jnp.int32),
            pltpu.VMEM((WID,), BF16),
            pltpu.VMEM((4, 4, 2, 32, 2 * WID), BF16),
            pltpu.VMEM((BACK, WID), BF16),
            pltpu.VMEM((512, WID), BF16),
            pltpu.VMEM((4, 4, 4, 16, COLS), BF16),
            pltpu.VMEM((4, 6, 2, 16, widths[0]), BF16),
            pltpu.VMEM((4, 6, 2, 16, widths[1]), BF16),
            pltpu.VMEM((4, 3, 16, widths[0]), BF16),
            pltpu.VMEM((4, 3, 16, widths[1]), BF16),
            pltpu.VMEM((4, 4, 4, 16, COLS), BF16),
            pltpu.VMEM((4, 2, 4, 32, 2 * WID), BF16),
            pltpu.VMEM((4, 4, 32, 2 * WID), BF16),
            pltpu.VMEM((4, 4, 32, 2 * WID), BF16),
            pltpu.VMEM((15, 32, 2 * WID), BF16),
            pltpu.SemaphoreType.DMA((COPIES,)),
            pltpu.SemaphoreType.DMA((COPIES,)),
            pltpu.SemaphoreType.DMA((7,)),
        ],
        compiler_params=pltpu.CompilerParams(collective_id=0, has_side_effects=True, vmem_limit_bytes=48 << 20),
        name="swiglu_layer",
    )(*here)
    out, grad, gg, gu, gd = pl.pallas_call(
        deliver,
        out_shape=(
            jax.ShapeDtypeStruct((32, WID), BF16),
            jax.ShapeDtypeStruct((32, WID), BF16),
            jax.ShapeDtypeStruct((HID, WID), F32),
            jax.ShapeDtypeStruct((HID, WID), F32),
            jax.ShapeDtypeStruct((HID, WID), F32),
        ),
        in_specs=[vmem] * 3,
        out_specs=[hbm] * 5,
        scratch_shapes=[pltpu.SemaphoreType.DMA((5,))],
        compiler_params=pltpu.CompilerParams(vmem_limit_bytes=2 << 20),
        name="deliver",
    )(acts, joined, down)
    return out, grad, gg.T, gu.T, gd


def solution(mesh):
    in_specs = (
        P("tensor", "dp"),
        P("tensor", None),
        P("dp"),
        P("dp", "tensor"),
        P("dp", "tensor"),
        P("tensor", "dp"),
        P("tensor", "dp"),
    )
    out_specs = (
        P("tensor", "dp"),
        P("tensor", "dp"),
        P("dp", "tensor"),
        P("dp", "tensor"),
        P("tensor", "dp"),
    )
    return jax.shard_map(shards, mesh=mesh, in_specs=in_specs, out_specs=out_specs, check_vma=False)
```
